128 devices in a mesh: dp: 16 (over z_lo, x, core), feat: 8 (over z_hi, y).
Axes of the slice: x: 4, y: 4, z: 4 (z_hi: 2, z_lo: 2; z = z_hi * 2 + z_lo), core: 2. Of those that a mesh axis runs over, the one named last changes fastest.
Arguments:
- embeddings: bfloat16 [2560, 128, 128], P('dp', 'feat'), may hold values from -8 to 8
- proj_weight: bfloat16 [128, 16], P('feat'), may hold values from -0.046875 to 0.046875
- up_weight: bfloat16 [2048, 8192], P('dp', 'feat'), may hold values from -0.125 to 0.125
- down_weight: bfloat16 [8192, 4096], P('feat', 'dp'), may hold values from -0.0625 to 0.0625
- mix_weight: bfloat16 [128, 96], P(None, 'feat'), may hold values from -0.5 to 0.5
- out_gain: float32 [128], replicated, may hold values from 0.1 to 1.9
- cotangent: bfloat16 [2560, 128, 128], P('dp', 'feat'), may hold values from -6 to 6
Outputs:
- layer_out: bfloat16 [2560, 128, 128], P('dp', 'feat')
- gain_grad: float32 [128], replicated
- mix_grad: float32 [128, 96], P(None, 'feat')
- up_grad: bfloat16 [2048, 8192], P('dp', 'feat')
- down_grad: bfloat16 [8192, 4096], P('feat', 'dp')
- proj_grad: float32 [128, 16], P('feat')
The draws below stay inside these ranges and needn't reach their ends.
All inputs are finite; a program needn't handle non-finite values.
Results may differ from the reference program's by a relative error of at most 0.03.
Values may be sent and summed in bfloat16 or wider, within the bound.
No kernel may reach another device: no remote copies, remote signals or barrier semaphores. Data moves between devices by JAX's collectives and lax.ppermute only.
A program may use at most 128 MiB of HBM per device.

```python
import jax
import jax.numpy as jnp
from jax import lax

D = 128
N = 128
K = 16
HID = 8192
NF = 32
NL = 96
B = 2560
N_DP = 16
N_FEAT = 8


def draw_embeddings(key, part):
    key = jax.random.fold_in(key, 11)
    first, second = jax.random.split(key, 2)
    ramp = jnp.exp(jnp.log(3.0) * jnp.arange(N, dtype=jnp.float32) / (N - 1))
    base = jax.random.normal(first, (B, N, D), jnp.float32)
    scale = jnp.exp(jax.random.uniform(second, (B, 1, 1), jnp.float32, jnp.log(0.5), jnp.log(1.5)))
    values = base * scale * ramp[None, :, None]
    return jnp.clip(values, -8.0, 8.0).astype(jnp.bfloat16)


def levels(rng, shape, shards, smallest, largest):
    def one(position, blocks):
        steps = jax.random.uniform(jax.random.fold_in(jax.random.fold_in(rng, 6), position), (blocks,), jnp.float32, smallest / len(shards), largest / len(shards))
        return jnp.repeat(jnp.exp(steps), shape[position] // blocks).reshape((-1,) + (1,) * (len(shape) - position - 1))

    gain = one(*shards[0])
    for cut in shards[1:]:
        gain = gain * one(*cut)
    return gain


def gaussian(rng, extent, spread, limit, cuts=(), kind=jnp.bfloat16):
    drawn = spread * jax.random.normal(rng, extent, jnp.float32)
    if cuts:
        drawn = drawn * levels(rng, extent, cuts, -0.22, 0.18)
    return jnp.clip(drawn, -limit, limit).astype(kind)


def setup_inputs(seed: int = 0) -> dict:
    seeds = jax.random.split(jax.random.key(seed), 8)
    return {
        "embeddings": draw_embeddings(jax.random.fold_in(seeds[7], 71), 0),
        "proj_weight": gaussian(seeds[1], (N, K), (N * D) ** -0.5, 0.046875, ((0, 8),)),
        "up_weight": gaussian(seeds[2], (N * K, HID), (N * K) ** -0.5, 0.125, ((0, 16), (1, 8))),
        "down_weight": gaussian(seeds[3], (HID, NF * D), HID ** -0.5, 0.0625, ((0, 8), (1, 16))),
        "mix_weight": gaussian(seeds[4], (N, NL), N ** -0.5, 0.5, ((1, 8),)),
        "out_gain": jnp.clip(1.0 + 0.18 * jax.random.normal(seeds[5], (D,), jnp.float32), 0.1, 1.9),
        "cotangent": gaussian(seeds[6], (B, N, D), 1.0, 6.0, ((0, 16), (1, 8))),
    }


def silu_slope(value):
    sig = jax.nn.sigmoid(value)
    return sig * (1.0 + value * (1.0 - sig))

def grouped_product(left, right, groups):
    left_blocks = left.reshape(groups, -1, left.shape[1])
    right_blocks = right.reshape(groups, -1, right.shape[1])

    def step(total, pair):
        term = jnp.dot(pair[0].T, pair[1], preferred_element_type=jnp.float32).astype(jnp.bfloat16)
        term = lax.optimization_barrier(term)
        return (total + term.astype(jnp.float32), None)
    start = jnp.zeros((left.shape[1], right.shape[1]), jnp.float32)
    total, unused = lax.scan(step, start, (left_blocks, right_blocks))
    return total.astype(jnp.bfloat16)

def reference(embeddings, proj_weight, up_weight, down_weight, mix_weight, out_gain, cotangent):
    samples = embeddings.shape[0]
    xfull = embeddings.astype(jnp.float32)
    proj = jnp.einsum('bnd,nk->bdk', xfull, proj_weight.astype(jnp.float32))
    proj_b = proj.astype(jnp.bfloat16)
    inter = jnp.einsum('bnd,bdk->bnk', xfull, proj_b.astype(jnp.float32)).reshape(samples, N * K)
    mean1 = lax.optimization_barrier(jnp.mean(inter, axis=1, keepdims=True))
    cent1 = inter - mean1
    rstd1 = lax.rsqrt(lax.optimization_barrier(jnp.mean(cent1 * cent1, axis=1, keepdims=True)) + 1e-05)
    normal1 = cent1 * rstd1
    normed_b = normal1.astype(jnp.bfloat16)
    pre = jnp.dot(normed_b, up_weight, preferred_element_type=jnp.float32)
    hidden_b = jax.nn.silu(pre).astype(jnp.bfloat16)
    fmb = jnp.dot(hidden_b, down_weight, preferred_element_type=jnp.float32)
    lcb = jnp.einsum('bnd,nl->bld', xfull, mix_weight.astype(jnp.float32))
    fmb_groups = fmb.reshape(samples, N_FEAT, NF // N_FEAT, D)
    lcb_groups = lcb.reshape(samples, N_FEAT, NL // N_FEAT, D)
    joined = jnp.concatenate([fmb_groups, lcb_groups], axis=2).reshape(samples, N, D)
    summed = joined + xfull
    mean2 = lax.optimization_barrier(jnp.mean(summed, axis=2, keepdims=True))
    cent2 = summed - mean2
    rstd2 = lax.rsqrt(lax.optimization_barrier(jnp.mean(cent2 * cent2, axis=2, keepdims=True)) + 1e-05)
    normal2 = cent2 * rstd2
    layer_out = (normal2 * out_gain).astype(jnp.bfloat16)
    cotan = cotangent.astype(jnp.float32)
    gain_grad = lax.optimization_barrier(jnp.sum(cotan * normal2, axis=(0, 1)))
    dnorm = cotan * out_gain
    dsum = rstd2 * (dnorm - lax.optimization_barrier(jnp.mean(dnorm, axis=2, keepdims=True)) - normal2 * lax.optimization_barrier(jnp.mean(dnorm * normal2, axis=2, keepdims=True)))
    dsum_groups = dsum.reshape(samples, N_FEAT, N // N_FEAT, D)
    d_fmb = dsum_groups[:, :, :NF // N_FEAT].reshape(samples, NF * D)
    d_lcb = dsum_groups[:, :, NF // N_FEAT:].reshape(samples, NL, D)
    mix_grad = jnp.einsum('bnd,bld->nl', xfull, d_lcb)
    d_fmb_b = d_fmb.astype(jnp.bfloat16)
    down_grad = grouped_product(hidden_b, d_fmb_b, N_DP)
    d_hidden = jnp.dot(d_fmb_b, down_weight.T, preferred_element_type=jnp.float32)
    d_pre_b = (d_hidden * silu_slope(pre)).astype(jnp.bfloat16)
    up_grad = grouped_product(normed_b, d_pre_b, N_DP)
    d_normed = jnp.dot(d_pre_b, up_weight.T, preferred_element_type=jnp.float32)
    d_inter = rstd1 * (d_normed - lax.optimization_barrier(jnp.mean(d_normed, axis=1, keepdims=True)) - normal1 * lax.optimization_barrier(jnp.mean(d_normed * normal1, axis=1, keepdims=True)))
    d_inter = d_inter.reshape(samples, N, K)
    d_proj = jnp.einsum('bnd,bnk->bdk', xfull, d_inter)
    proj_grad = jnp.einsum('bnd,bdk->nk', xfull, d_proj)
    return (layer_out, gain_grad, mix_grad, up_grad, down_grad, proj_grad)
```

```python
import jax
import jax.numpy as jnp
from jax import lax
from jax.sharding import Mesh, PartitionSpec as P

BF = jnp.bfloat16
F32 = jnp.float32
DP = ("zlo", "x", "core")
FEAT = ("zhi", "y")
ALL = DP + FEAT
EPS = 1e-05
FWD = [(i, (i + 1) % 4) for i in range(4)]
BWD = [(i, (i + 3) % 4) for i in range(4)]
SWAP = [(0, 1), (1, 0)]


def silu_slope(value):
    sig = jax.nn.sigmoid(value)
    return sig * (1.0 + value * (1.0 - sig))


def sibling(a):
    return lax.ppermute(a, "core", SWAP)


def across(a):
    return lax.ppermute(a, "zlo", SWAP)


def right(a):
    return lax.ppermute(a, "x", FWD)


def left(a):
    return lax.ppermute(a, "x", BWD)


def exchange(a, axes):
    return lax.all_to_all(a, axes, 0, 0, tiled=True)


def flip(a, axis, position):
    return jnp.where(position == 0, a, jnp.flip(a, axis))


def turn(a, axis, by):
    return lax.dynamic_slice_in_dim(jnp.concatenate([a, a], axis), by, 4, axis)


def to_relative(a):
    rows, cols = a.shape
    a = a.reshape(rows, 2, 4, 2, cols // 16)
    a = flip(a, 1, lax.axis_index("zlo"))
    a = turn(a, 2, lax.axis_index("x"))
    return a.reshape(rows, cols)


def to_absolute(a):
    rows, cols = a.shape
    a = a.reshape(rows, 2, 4, 2, cols // 16)
    a = flip(a, 1, lax.axis_index("zlo"))
    a = turn(a, 2, lax.rem(4 - lax.axis_index("x"), 4))
    return a.reshape(rows, cols)


def by_core(core, mine, theirs, axis):
    return jnp.where(
        core == 0,
        jnp.concatenate([mine, theirs], axis),
        jnp.concatenate([theirs, mine], axis),
    )


def gather_weights(up, down):
    core = lax.axis_index("core")

    def up_half(which):
        return lax.dynamic_slice_in_dim(up, which * 512, 512, 1)

    def down_half(which):
        return lax.dynamic_slice_in_dim(down, which * 512, 512, 0)

    up_chip = by_core(core, up_half(core), sibling(up_half(1 - core)), 0)
    down_chip = by_core(core, down_half(core), sibling(down_half(1 - core)), 1)
    mine = jnp.concatenate([up_chip, down_chip], 0)
    half = mine.shape[0] // 2

    def around(a):
        from_left, from_right = right(a), left(a)
        far = jnp.concatenate([right(from_left[:half]), left(from_right[half:])], 0)
        return [a, from_right, far, from_left]

    other = across(mine)
    return around(mine) + around(other)


def reduce_weights(pieces):
    half = pieces[0].shape[0] // 2

    def plus(*terms):
        total = terms[0].astype(F32)
        for term in terms[1:]:
            total = total + term.astype(F32)
        return total.astype(BF)

    def around(own, plus_one, far, minus_one):
        from_left = right(far[:half])
        from_right = left(far[half:])
        direct_left = right(plus_one[half:])
        direct_right = left(minus_one[:half])
        relay_left = right(plus(plus_one[:half], from_left))
        relay_right = left(plus(minus_one[half:], from_right))
        return jnp.concatenate(
            [
                plus(own[:half], direct_right, relay_left),
                plus(own[half:], direct_left, relay_right),
            ],
            0,
        )

    other = across(around(*pieces[4:]))
    total = plus(around(*pieces[:4]), other)
    up_chip, down_chip = total[:256], total[256:]
    core = lax.axis_index("core")

    def up_rows(which):
        return lax.dynamic_slice_in_dim(up_chip, which * 128, 128, 0)

    def down_cols(which):
        return lax.dynamic_slice_in_dim(down_chip, which * 256, 256, 1)

    up_grad = by_core(core, up_rows(core), sibling(up_rows(1 - core)), 1)
    down_grad = by_core(core, down_cols(core), sibling(down_cols(1 - core)), 0)
    return up_grad, down_grad


def dot(a, b, dims):
    return lax.dot_general(a, b, (dims, ((), ())), preferred_element_type=F32)


def per_device(embeddings, proj_weight, up_weight, down_weight, mix_weight, out_gain, cotangent):
    weights = gather_weights(up_weight, down_weight)
    up_all = jnp.concatenate([w[:256] for w in weights], 0)
    down_all = jnp.concatenate([w[256:] for w in weights], 1)

    def spread(a):
        return jnp.broadcast_to(a.reshape(1, -1, 128), (8, a.size // 128, 128))

    message = jnp.concatenate(
        [
            embeddings.reshape(8, 320, 128),
            cotangent.reshape(8, 320, 128),
            spread(mix_weight.T),
            spread(proj_weight),
            jnp.zeros((8, 2, 128), BF),
        ],
        1,
    )
    message = exchange(message, FEAT)
    tokens = message[:, :320].reshape(8, 20, 16, 128).transpose(1, 0, 2, 3).reshape(20, 128, 128)
    cotan = message[:, 320:640].reshape(8, 20, 16, 128).transpose(1, 0, 2, 3).astype(F32)
    mix = message[:, 640:652].reshape(96, 128)
    proj_w = message[:, 652:654].reshape(128, 16)

    proj = jnp.einsum("nk,bnd->bkd", proj_w, tokens, preferred_element_type=F32).astype(BF)
    inter = jnp.einsum("bkd,bnd->bkn", proj, tokens, preferred_element_type=F32)
    cent1 = inter - jnp.mean(inter, axis=(1, 2), keepdims=True)
    rstd1 = lax.rsqrt(jnp.mean(cent1 * cent1, axis=(1, 2), keepdims=True) + EPS)
    normal1 = cent1 * rstd1
    normed = to_relative(normal1.astype(BF).transpose(0, 2, 1).reshape(20, 2048))

    normed = exchange(jnp.broadcast_to(normed[None], (8, 20, 2048)), FEAT).reshape(160, 2048)
    normed = jnp.concatenate([normed, sibling(normed)], 0)
    pre = dot(normed, up_all, ((1,), (0,)))
    hidden = jax.nn.silu(pre).astype(BF)
    fmb = dot(hidden, down_all, ((1,), (0,)))
    fmb = (fmb[:160] + sibling(fmb[160:].astype(BF)).astype(F32)).astype(BF)
    fmb = jnp.sum(exchange(fmb.reshape(8, 20, 4096), FEAT).astype(F32), 0)
    fmb = to_absolute(fmb).reshape(20, 8, 4, 128)

    lcb = jnp.einsum("jn,bnd->bjd", mix, tokens, preferred_element_type=F32)
    summed = jnp.concatenate([fmb, lcb.reshape(20, 8, 12, 128)], 2)
    summed = summed + tokens.reshape(20, 8, 16, 128).astype(F32)
    cent2 = summed - jnp.mean(summed, axis=3, keepdims=True)
    rstd2 = lax.rsqrt(jnp.mean(cent2 * cent2, axis=3, keepdims=True) + EPS)
    normal2 = cent2 * rstd2
    layer_out = (normal2 * out_gain).astype(BF)
    gain_part = jnp.sum(cotan * normal2, axis=(0, 1, 2))
    dnorm = cotan * out_gain
    dsum = rstd2 * (
        dnorm
        - jnp.mean(dnorm, axis=3, keepdims=True)
        - normal2 * jnp.mean(dnorm * normal2, axis=3, keepdims=True)
    )
    d_fmb = to_relative(dsum[:, :, :4].astype(BF).reshape(20, 4096))
    d_lcb = dsum[:, :, 4:].astype(BF).reshape(20, 96, 128)

    d_fmb = exchange(jnp.broadcast_to(d_fmb[None], (8, 20, 4096)), FEAT).reshape(160, 4096)
    d_fmb = jnp.concatenate([d_fmb, sibling(d_fmb)], 0)
    d_hidden = dot(d_fmb, down_all, ((1,), (1,)))
    d_pre = (d_hidden * silu_slope(pre)).astype(BF)
    up_part = dot(normed, d_pre, ((0,), (0,))).astype(BF)
    down_part = dot(hidden, d_fmb, ((0,), (0,))).astype(BF)
    pieces = [
        jnp.concatenate(
            [up_part[r * 256 : (r + 1) * 256], down_part[:, r * 512 : (r + 1) * 512]], 0
        )
        for r in range(8)
    ]
    up_grad, down_grad = reduce_weights(pieces)

    d_normed = dot(d_pre, up_all, ((1,), (1,)))
    d_normed = (d_normed[:160] + sibling(d_normed[160:].astype(BF)).astype(F32)).astype(BF)
    message = jnp.concatenate(
        [
            d_normed.reshape(8, 320, 128),
            layer_out.transpose(1, 0, 2, 3).reshape(8, 320, 128),
        ],
        1,
    )
    message = exchange(message, FEAT)
    layer_out = message[:, 320:].reshape(160, 16, 128)
    d_normed = jnp.sum(message[:, :320].astype(F32), 0).reshape(20, 2048)
    d_normed = to_absolute(d_normed).reshape(20, 128, 16).transpose(0, 2, 1)
    d_inter = rstd1 * (
        d_normed
        - jnp.mean(d_normed, axis=(1, 2), keepdims=True)
        - normal1 * jnp.mean(d_normed * normal1, axis=(1, 2), keepdims=True)
    )
    d_proj = jnp.einsum(
        "bkn,bnd->bkd", d_inter.astype(BF), tokens, preferred_element_type=F32
    ).astype(BF)
    proj_part = jnp.einsum("bnd,bkd->nk", tokens, d_proj, preferred_element_type=F32)
    mix_part = jnp.einsum("bjd,bnd->jn", d_lcb, tokens, preferred_element_type=F32)

    last = jnp.concatenate(
        [
            proj_part.reshape(8, 2, 128),
            mix_part.reshape(8, 12, 128),
            jnp.broadcast_to(gain_part, (8, 1, 128)),
            jnp.zeros((8, 1, 128), F32),
        ],
        1,
    ).astype(BF)
    last = jnp.broadcast_to(last[None], (16, 8, 16, 128)).reshape(128, 16, 128)
    last = jnp.sum(exchange(last, ALL).astype(F32), 0)
    proj_grad = last[:2].reshape(16, 16)
    mix_grad = last[2:14].T
    gain_grad = last[14]
    return (layer_out, gain_grad, mix_grad, up_grad, down_grad, proj_grad)


def solution(mesh):
    grid = Mesh(mesh.devices.reshape(2, 4, 2, 2, 4), ALL)
    placed = (
        P(DP, FEAT, None),
        P(FEAT, None),
        P(DP, FEAT),
        P(FEAT, DP),
        P(None, FEAT),
        P(),
        P(DP, FEAT, None),
    )
    return jax.shard_map(
        per_device,
        mesh=grid,
        in_specs=placed,
        out_specs=(
            P(DP, FEAT, None),
            P(),
            P(None, FEAT),
            P(DP, FEAT),
            P(FEAT, DP),
            P(FEAT, None),
        ),
        check_vma=False,
    )
```

```python
import jax
import jax.numpy as jnp
from jax import lax
from jax.experimental import pallas as pl
from jax.experimental.pallas import tpu as pltpu
from jax.sharding import Mesh, PartitionSpec as P

BF = jnp.bfloat16
F32 = jnp.float32
DP = ("zlo", "x", "core")
FEAT = ("zhi", "y")
ALL = DP + FEAT
EPS = 1e-05
FWD = [(i, (i + 1) % 4) for i in range(4)]
BWD = [(i, (i + 3) % 4) for i in range(4)]
SWAP = [(0, 1), (1, 0)]
OWN, CORE, CHIP = 20, 160, 320


def sibling(a):
    return lax.ppermute(a, "core", SWAP)


def across(a):
    return lax.ppermute(a, "zlo", SWAP)


def right(a):
    return lax.ppermute(a, "x", FWD)


def left(a):
    return lax.ppermute(a, "x", BWD)


def exchange(a, axes):
    return lax.all_to_all(a, axes, 0, 0, tiled=True)


def together(*arrays):
    return lax.optimization_barrier(arrays)


def dot(a, b, dims):
    return lax.dot_general(a, b, (dims, ((), ())), preferred_element_type=F32)


def shape(dims, dtype=BF):
    return jax.ShapeDtypeStruct(dims, dtype)


def call(body, outs, *args, scratch=(), scalars=0, remote_in=0, remote_out=0, room=16):
    whole = pl.BlockSpec(memory_space=pltpu.VMEM)
    small = pl.BlockSpec(memory_space=pltpu.SMEM)
    there = pl.BlockSpec(memory_space=pl.ANY)
    return pl.pallas_call(
        body,
        out_shape=outs,
        in_specs=[small] * scalars
        + [whole] * (len(args) - scalars - remote_in)
        + [there] * remote_in,
        out_specs=[there] * remote_out + [whole] * (len(outs) - remote_out),
        scratch_shapes=list(scratch),
        compiler_params=pltpu.CompilerParams(vmem_limit_bytes=room * 1024 * 1024),
    )(*args)


def one_where(dims, test):
    rows = lax.broadcasted_iota(jnp.int32, dims, 0)
    cols = lax.broadcasted_iota(jnp.int32, dims, 1)
    return test(rows, cols).astype(F32).astype(BF)


def many(start, size):
    return pl.ds(pl.multiple_of(start, size), size)


def halves(core, width):
    return many(core * width, width), many((1 - core) * width, width)


def chip_rows(core):
    return one_where((256, 128), lambda r, c: r == (c % 16) * 16 + core * 8 + c // 16)


def send_kernel(place, up, down, sent, sems):
    unused, other = halves(place[0], 512)
    low, high = many((1 - place[0]) * 512, 256), many((1 - place[0]) * 512 + 256, 256)
    copies = [
        pltpu.make_async_copy(up.at[:, other], sent.at[pl.ds(0, 128)], sems.at[0]),
        pltpu.make_async_copy(
            down.at[low], sent.at[pl.ds(128, 256), pl.ds(0, 256)], sems.at[1]
        ),
        pltpu.make_async_copy(
            down.at[high], sent.at[pl.ds(128, 256), pl.ds(256, 256)], sems.at[2]
        ),
    ]
    for copy in copies:
        copy.start()
    for copy in copies:
        copy.wait()


def message_kernel(place, proj, mix, token, emb, message, sems):
    copy = pltpu.make_async_copy(emb, message.at[:, pl.ds(0, 320)], sems.at[0])
    copy.start()
    here = one_where((16, 128), lambda n, lane: lane == place[3] * 16 + n)
    proj_rows = dot(proj[...], here, ((0,), (0,))).astype(BF)
    shift = one_where((16, 12), lambda u, c: u == c + 4)
    mix_rows = dot(shift, mix[...], ((1,), (0,))).astype(BF)
    for group in range(8):
        message[group, 320:336] = proj_rows
        message[group, 336:352] = mix_rows
    copy.wait()


def piece_kernel(place, got, up, down, piece, mine_up, mine_down, sems):
    core = place[0]
    mine, unused = halves(core, 512)
    copies = [
        pltpu.make_async_copy(up.at[:, mine], mine_up, sems.at[0]),
        pltpu.make_async_copy(down.at[mine], mine_down, sems.at[1]),
    ]
    for copy in copies:
        copy.start()
    mine_at, other_at = halves(core, 256)
    piece[16:32, :, other_at] = got[128:, :256].reshape(16, 16, 256)
    piece[32:, :, other_at] = got[128:, 256:].reshape(16, 16, 256)
    rows = dot(chip_rows(1 - core), got[:128], ((1,), (0,)))
    copies[0].wait()
    rows += dot(chip_rows(core), mine_up[...], ((1,), (0,)))
    piece[:16] = rows.astype(BF).reshape(16, 16, 512)
    copies[1].wait()
    piece[16:, :, mine_at] = mine_down[...].reshape(32, 16, 256)


def total_of(refs):
    total = refs[0][...].astype(F32)
    for ref in refs[1:]:
        total += ref[...].astype(F32)
    return total.astype(BF)


def add_kernel(*refs):
    refs[-1][...] = total_of(refs[:-1])


def add(*terms):
    return call(add_kernel, [shape(terms[0].shape)], *terms)[0]


def add_both_kernel(own, from_right, relayed, minus, returned, over, on):
    over[...] = total_of((own, from_right, relayed))
    on[...] = total_of((minus, returned))


def join_kernel(own, got, layer, out):
    out[:, :16] = total_of((own, got))
    out[:, 16:] = layer[...]


def split_kernel(place, own, one, two, three, up_kept, down_kept, sent):
    core = place[0]
    total = total_of((own, one, two, three))
    up, down = total[:16].reshape(256, 512), total[16:].reshape(512, 512)
    up_kept[...] = dot(chip_rows(core), up, ((0,), (0,))).astype(BF)
    sent[:128] = dot(chip_rows(1 - core), up, ((0,), (0,))).astype(BF)
    first, second = down[:, :256], down[:, 256:]
    down_kept[...] = jnp.where(core == 0, first, second)
    other = jnp.where(core == 0, second, first)
    sent[128:, :256] = other[:256]
    sent[128:, 256:] = other[256:]


def finish_kernel(place, up_kept, down_kept, got, up, down):
    mine, other = halves(place[0], 512)
    up[:, mine] = up_kept[...]
    up[:, other] = got[:128]
    down[mine, :] = down_kept[...]
    down[other, :] = jnp.concatenate([got[128:, :256], got[128:, 256:]], 0)


def unpack(ref, width, start, size):
    quarter = start // (width // 4)
    tail = width + start - quarter * (width // 4)
    rest = ref[:, :16, tail : tail + size].astype(F32)
    rest = [rest[f, 4 * quarter : 4 * quarter + 4] for f in range(8)]
    rest = jnp.concatenate(rest, 0).astype(BF)
    return [ref[:, :16, start : start + size].reshape(128, size), rest]


def pack(part, ref, tails, width, start, size):
    quarter = start // (width // 4)
    tail = start - quarter * (width // 4)
    ref[:, :, start : start + size] = part[:128].astype(BF).reshape(8, 16, size)
    for f in range(8):
        row = 16 * f + 4 * quarter
        tails[row : row + 4, tail : tail + size] = part[128 + 4 * f : 132 + 4 * f]
    if quarter == 3:
        rest = tails[:, tail : tail + size].astype(BF)
        ref[:, :, width + tail : width + tail + size] = rest.reshape(8, 16, size)


def chip_of(place, r):
    return jnp.bitwise_xor(place[1], r // 4) * 4 + lax.rem(place[2] + r % 4, 4)


def second_part(piece):
    if len(piece) == 1:
        return piece[0][16:].reshape(512, 512)
    low, high = piece
    return jnp.concatenate([low[16:].reshape(128, 512), high[...].reshape(384, 512)], 0)


def pieces_of(refs, late, sems):
    a, b, c, d, e, f, g, h, low, high = refs
    copies = [
        pltpu.make_async_copy(low, late.at[pl.ds(0, 24)], sems.at[0]),
        pltpu.make_async_copy(high, late.at[pl.ds(24, 24)], sems.at[1]),
    ]
    for copy in copies:
        copy.start()
    return [(0, [a]), (1, [b]), (2, [c, d]), (3, [e]), (4, [f]), (5, [g]), (7, [h]), (6, [late])], copies


def features_kernel(message, cot, payload, normal, rstds, tails):
    for b in range(OWN):
        payload[:, 16:, 128 * b : 128 * b + 128] = cot[:, 16 * b : 16 * b + 16]
    proj_w = message[0, 320:336].astype(F32)
    for f in range(1, 8):
        proj_w += message[f, 320:336].astype(F32)
    proj_w = proj_w.astype(BF)

    def sample(b, carry):
        tokens = message[:, many(b * 16, 16)].reshape(128, 128)
        proj = dot(proj_w, tokens, ((1,), (0,))).astype(BF)
        inter = dot(proj, tokens, ((1,), (1,)))
        cent = inter - jnp.sum(inter, keepdims=True) * (1.0 / 2048)
        rstd = lax.rsqrt(jnp.sum(cent * cent, keepdims=True) * (1.0 / 2048) + EPS)
        normal[b] = cent * rstd
        rstds[b] = jnp.broadcast_to(rstd, (16, 128))
        return carry

    lax.fori_loop(0, OWN, sample, 0, unroll=5)
    for k in range(16):
        block = normal[:, k, :]
        quarter, tail = k // 4 * 4, k % 4 * 128
        tails[quarter : quarter + 4, tail : tail + 128] = block[16:]
        block = block[:16].astype(BF)
        for f in range(8):
            payload[f, :16, 128 * k : 128 * k + 128] = block
    block = tails[...].astype(BF)
    for f in range(8):
        payload[f, :16, 2048:] = block


def forward_kernel(place, own, sib, *refs):
    hidden, pre, rows, held, fmb_own, fmb_sib, tail_own, tail_sib, late, sems = refs[10:]
    weights, copies = pieces_of(refs[:10], late, sems)
    for r, piece in weights:
        if r == 6:
            for copy in copies:
                copy.wait()
        held[:, many(chip_of(place, r) * 16, 16)] = piece[0][:16]
    total = jnp.zeros((CHIP, 512), F32)
    for j in range(8):
        part = unpack(own, 2048, 256 * j, 256) + unpack(sib, 2048, 256 * j, 256)
        part = jnp.concatenate(part, 0)
        rows[:, 256 * j : 256 * j + 256] = part
        matrix = held[2 * j : 2 * j + 2].reshape(256, 512)
        total += dot(part, matrix, ((1,), (0,)))
    pre[...] = total
    act = (total / (1.0 + jnp.exp(-total))).astype(BF)
    hidden[...] = act
    for r, piece in sorted(weights, key=lambda item: item[0]):
        part = dot(act, second_part(piece), ((1,), (0,)))
        pack(part[:CORE], fmb_own, tail_own, 4096, 512 * r, 512)
        pack(part[CORE:], fmb_sib, tail_sib, 4096, 512 * r, 512)


def backward_kernel(place, d_own, d_sib, rows, hidden, pre, held, *refs):
    grads, (dn_own, dn_sib) = refs[10:18], refs[18:20]
    d_rows, made, made_down, tail_own, tail_sib, late, sems, out_sems = refs[20:]
    weights, copies = pieces_of(refs[:10], late, sems)
    total = jnp.zeros((CHIP, 512), F32)
    for r, piece in weights:
        part = unpack(d_own, 4096, 512 * r, 512) + unpack(d_sib, 4096, 512 * r, 512)
        part = jnp.concatenate(part, 0)
        d_rows[:, 512 * r : 512 * r + 512] = part
        if r == 6:
            for copy in copies:
                copy.wait()
        total += dot(part, second_part(piece), ((1,), (1,)))
    sends = []

    def send(source, there, sem):
        sends.append(pltpu.make_async_copy(source, there, out_sems.at[sem]))
        sends[-1].start()

    act = hidden[...].T
    for r in (6, 7, 2, 5, 4, 1, 3, 0):
        part = dot(act, d_rows[:, 512 * r : 512 * r + 512], ((1,), (0,)))
        made_down[r] = part.astype(BF).reshape(32, 16, 512)
        send(made_down.at[r], grads[r].at[pl.ds(16, 32)], 8 + r)
    sig = 1.0 / (1.0 + jnp.exp(-pre[...]))
    d_pre = (total * (sig * (1.0 + pre[...] * (1.0 - sig)))).astype(BF)
    for j in range(8):
        part = dot(rows[:, 256 * j : 256 * j + 256], d_pre, ((0,), (0,)))
        made[2 * j : 2 * j + 2] = part.astype(BF).reshape(2, 128, 512)
    for r in range(8):
        send(made.at[:, many(chip_of(place, r) * 16, 16)], grads[r].at[pl.ds(0, 16)], r)
    for j in range(8):
        part = dot(d_pre, held[2 * j : 2 * j + 2].reshape(256, 512), ((1,), (1,)))
        pack(part[:CORE], dn_own, tail_own, 2048, 256 * j, 256)
        pack(part[CORE:], dn_sib, tail_sib, 2048, 256 * j, 256)
    for copy in sends:
        copy.wait()


def norm_kernel(
    place, parts, message, cot, gain, layer, d_fmb, mix_part, gain_part, fm, grad, tails
):
    def added(cols):
        total = parts[0, :, cols].astype(F32)
        for f in range(1, 8):
            total += parts[f, :, cols].astype(F32)
        return total

    fm[...] = jnp.zeros_like(fm)
    tails[...] = added(slice(4096, 5120))
    for r in range(8):
        main = added(slice(512 * r, 512 * r + 512))
        quarter, tail = r // 2 * 4, r % 2 * 512
        for u in range(4):
            at = slice(128 * u, 128 * u + 128)
            fm[:16, chip_of(place, r), u, :] = main[:, at]
            at = slice(tail + 128 * u, tail + 128 * u + 128)
            fm[16:, chip_of(place, r), u, :] = tails[quarter : quarter + 4, at]
    mix_part[...] = jnp.zeros_like(mix_part)
    gain_part[...] = jnp.zeros_like(gain_part)
    scale = gain[...]
    mixing = message[:, 336:352].reshape(128, 128)

    def mean(a):
        return jnp.sum(a, axis=1, keepdims=True) * (1.0 / 128)

    def sample(b, carry):
        at = many(b * 16, 16)
        tokens = message[:, at].reshape(128, 128)
        cotan = cot[:, 16:, many(b * 128, 128)].reshape(128, 128).astype(F32)
        lcb = dot(mixing, tokens, ((1,), (0,)))
        summed = lcb + fm[b].reshape(128, 128) + tokens.astype(F32)
        cent = summed - mean(summed)
        rstd = lax.rsqrt(mean(cent * cent) + EPS)
        normal = cent * rstd
        layer[:, :, many(b * 128, 128)] = (normal * scale).astype(BF).reshape(8, 16, 128)
        gain_part[...] += jnp.sum((cotan * normal).reshape(16, 8, 128), axis=0)
        dnorm = cotan * scale
        dsum = rstd * (dnorm - mean(dnorm) - normal * mean(dnorm * normal))
        grad[b] = dsum.reshape(8, 16, 128)
        mix_part[...] += dot(dsum.astype(BF), tokens, ((1,), (1,)))
        return carry

    lax.fori_loop(0, OWN, sample, 0, unroll=5)
    for r in range(8):
        quarter, tail = r // 2 * 4, r % 2 * 512
        for u in range(4):
            block = grad[:, chip_of(place, r), u, :]
            at = slice(tail + 128 * u, tail + 128 * u + 128)
            tails[quarter : quarter + 4, at] = block[16:]
            block = block[:16].astype(BF)
            for f in range(8):
                d_fmb[f, :, 512 * r + 128 * u : 512 * r + 128 * u + 128] = block
    block = tails[...].astype(BF)
    for f in range(8):
        d_fmb[f, :, 4096:] = block


def last_kernel(back, normal, rstds, message, mix_part, gain_part, last, grad, proj_part):
    total = back[0, :16].astype(F32)
    for f in range(1, 8):
        total += back[f, :16].astype(F32)
    for k in range(16):
        quarter, tail = k // 4 * 4, 2048 + k % 4 * 128
        grad[:16, k, :] = total[:, 128 * k : 128 * k + 128]
        grad[16:, k, :] = total[quarter : quarter + 4, tail : tail + 128]
    proj_part[...] = jnp.zeros_like(proj_part)

    def sample(b, carry):
        tokens = message[:, many(b * 16, 16)].reshape(128, 128)
        d_normed, norm = grad[b], normal[b]
        first = jnp.sum(d_normed, keepdims=True) * (1.0 / 2048)
        second = jnp.sum(d_normed * norm, keepdims=True) * (1.0 / 2048)
        d_inter = rstds[b] * (d_normed - first - norm * second)
        d_proj = dot(d_inter.astype(BF), tokens, ((1,), (0,)))
        proj_part[...] += dot(d_proj.astype(BF), tokens, ((1,), (1,)))
        return carry

    lax.fori_loop(0, OWN, sample, 0, unroll=5)
    repeat = one_where((16, 128), lambda k, lane: lane % 16 == k)
    spread = dot(proj_part[...].astype(BF), repeat, ((0,), (0,)))
    token = lax.broadcasted_iota(jnp.int32, (128, 128), 0)
    lane = lax.broadcasted_iota(jnp.int32, (128, 128), 1)
    spread = jnp.where(token % 8 == lane // 16, spread, 0.0).astype(BF)
    collect = one_where(
        (128, 128), lambda r, n: (r % 16 < 2) & (n // 8 == (r // 16) * 2 + r % 16)
    )
    rows = dot(collect, spread, ((1,), (0,)))
    gain = jnp.sum(gain_part[...], axis=0, keepdims=True)
    rows += jnp.where(token % 16 == 2, jnp.broadcast_to(gain, (128, 128)), 0.0)
    rows += jnp.where(token % 16 >= 4, mix_part[...], 0.0)
    rows = rows.astype(BF).reshape(8, 16, 128)
    for d in range(16):
        last[8 * d : 8 * d + 8] = rows


def unfold_kernel(back, layer):
    for b in range(OWN):
        layer[:, b] = back[:, 16:, 128 * b : 128 * b + 128]


def finish_weights(place, own, from_left, relayed, other):
    up_kept, down_kept, sent = call(
        split_kernel,
        [shape((128, 512)), shape((512, 256)), shape((384, 512))],
        place,
        own,
        from_left,
        relayed,
        other,
        scalars=1,
    )
    return call(
        finish_kernel,
        [shape((128, 1024)), shape((1024, 256))],
        place,
        up_kept,
        down_kept,
        sibling(sent),
        scalars=1,
    )


def per_device(embeddings, proj_weight, up_weight, down_weight, mix_weight, out_gain, cotangent):
    place = jnp.stack(
        [lax.axis_index(axis) for axis in ("core", "zlo", "x")]
        + [lax.axis_index("zhi") * 4 + lax.axis_index("y")]
    ).astype(jnp.int32)
    (sent,) = call(
        send_kernel,
        [shape((384, 512))],
        place,
        up_weight,
        down_weight,
        scratch=[pltpu.SemaphoreType.DMA((3,))],
        scalars=1,
        remote_in=2,
        room=60,
    )
    (mine,) = call(
        piece_kernel,
        [shape((48, 16, 512))],
        place,
        sibling(sent),
        up_weight,
        down_weight,
        scratch=[
            pltpu.VMEM((128, 512), BF),
            pltpu.VMEM((512, 256), BF),
            pltpu.SemaphoreType.DMA((2,)),
        ],
        scalars=1,
        remote_in=2,
        room=60,
    )
    other = across(mine)
    near_left, near_right = right(mine), left(mine)
    (message,) = call(
        message_kernel,
        [shape((8, 352, 128))],
        place,
        proj_weight,
        mix_weight.T,
        sibling(mine[0]),
        embeddings.reshape(8, 320, 128),
        scratch=[pltpu.SemaphoreType.DMA((1,))],
        scalars=1,
        remote_in=1,
        room=60,
    )
    message = exchange(message, FEAT)
    message, near_left, near_right, other = together(message, near_left, near_right, other)
    other_left, other_right = right(other), left(other)
    far_low, far_high = right(near_left[:24]), left(near_right[24:])

    payload, normal1, rstd1 = call(
        features_kernel,
        [shape((8, 32, 2560)), shape((OWN, 16, 128), F32), shape((OWN, 16, 128), F32)],
        message,
        cotangent.reshape(8, 320, 128),
        scratch=[pltpu.VMEM((16, 512), F32)],
    )
    payload, far_low, far_high = together(payload, far_low, far_high)
    normed = exchange(payload, FEAT)
    normed, other_left, other_right = together(normed, other_left, other_right)
    other_low, other_high = right(other_left[:24]), left(other_right[24:])
    weights = [mine, near_right, far_low, far_high, near_left]
    weights += [other, other_right, other_left, other_low, other_high]
    hidden, pre, rows, first, fmb_own, fmb_sib = call(
        forward_kernel,
        [
            shape((CHIP, 512)),
            shape((CHIP, 512), F32),
            shape((CHIP, 2048)),
            shape((16, 128, 512)),
            shape((8, 16, 5120)),
            shape((8, 16, 5120)),
        ],
        place,
        normed,
        sibling(normed),
        *weights,
        scratch=[
            pltpu.VMEM((128, 1024), F32),
            pltpu.VMEM((128, 1024), F32),
            pltpu.VMEM((48, 16, 512), BF),
            pltpu.SemaphoreType.DMA((2,)),
        ],
        scalars=1,
        remote_in=2,
    )
    fmb = exchange(add(fmb_own, sibling(fmb_sib)), FEAT)

    layer_out, d_fmb, mix_part, gain_part = call(
        norm_kernel,
        [
            shape((8, 16, 2560)),
            shape((8, 16, 5120)),
            shape((128, 128), F32),
            shape((8, 128), F32),
        ],
        place,
        fmb,
        message,
        normed,
        out_gain.reshape(1, 128),
        scratch=[
            pltpu.VMEM((OWN, 8, 16, 128), F32),
            pltpu.VMEM((OWN, 8, 16, 128), F32),
            pltpu.VMEM((16, 1024), F32),
        ],
        scalars=1,
    )

    d_fmb = exchange(d_fmb, FEAT)
    outs = call(
        backward_kernel,
        [shape((48, 16, 512))] * 8 + [shape((8, 16, 2560))] * 2,
        place,
        d_fmb,
        sibling(d_fmb),
        rows,
        hidden,
        pre,
        first,
        *weights,
        scratch=[
            pltpu.VMEM((CHIP, 4096), BF),
            pltpu.VMEM((16, 128, 512), BF),
            pltpu.VMEM((8, 32, 16, 512), BF),
            pltpu.VMEM((128, 512), F32),
            pltpu.VMEM((128, 512), F32),
            pltpu.VMEM((48, 16, 512), BF),
            pltpu.SemaphoreType.DMA((2,)),
            pltpu.SemaphoreType.DMA((16,)),
        ],
        scalars=1,
        remote_in=2,
        remote_out=8,
        room=24,
    )
    own0, plus0, far0, minus0, own1, plus1, far1, minus1, dn_own, dn_sib = outs

    from_left, from_right = right(far1), left(minus1)
    (back,) = call(join_kernel, [shape((8, 32, 2560))], dn_own, sibling(dn_sib), layer_out)
    back = exchange(back, FEAT)
    from_left, from_right, far0 = together(from_left, from_right, far0)
    relayed, returned = right(add(plus1, from_left)), left(far0)
    (last,) = call(
        last_kernel,
        [shape((128, 16, 128))],
        back,
        normal1,
        rstd1,
        message,
        mix_part,
        gain_part,
        scratch=[pltpu.VMEM((OWN, 16, 128), F32), pltpu.VMEM((16, 128), F32)],
    )
    relayed, returned, plus0, last = together(relayed, returned, plus0, last)
    from_left = right(plus0)
    over, on = call(
        add_both_kernel,
        [shape((48, 16, 512))] * 2,
        own1,
        from_right,
        relayed,
        minus0,
        returned,
    )
    other, relayed = across(over), left(on)
    last = exchange(last, ALL)
    up_grad, down_grad = finish_weights(place, own0, from_left, relayed, other)
    up_grad, down_grad, last = together(up_grad, down_grad, last)
    (layer_out,) = call(unfold_kernel, [shape((8, OWN, 16, 128))], back)
    last = jnp.sum(last.astype(F32), 0)
    proj_grad = last[:2].reshape(16, 16)
    mix_grad = last[4:].T
    gain_grad = last[2]
    layer_out = layer_out.reshape(160, 16, 128)
    return (layer_out, gain_grad, mix_grad, up_grad, down_grad, proj_grad)


def solution(mesh):
    grid = Mesh(mesh.devices.reshape(2, 4, 2, 2, 4), ALL)
    placed = (
        P(DP, FEAT, None),
        P(FEAT, None),
        P(DP, FEAT),
        P(FEAT, DP),
        P(None, FEAT),
        P(),
        P(DP, FEAT, None),
    )
    return jax.shard_map(
        per_device,
        mesh=grid,
        in_specs=placed,
        out_specs=(
            P(DP, FEAT, None),
            P(),
            P(None, FEAT),
            P(DP, FEAT),
            P(FEAT, DP),
            P(FEAT, None),
        ),
        check_vma=False,
    )
```

```python
import functools

import jax
import jax.numpy as jnp
from jax import lax
from jax.experimental import pallas as pl
from jax.experimental.pallas import tpu as pltpu
from jax.sharding import Mesh, PartitionSpec as P

BF = jnp.bfloat16
F32 = jnp.float32
DP = ("zlo", "x", "core")
FEAT = ("zhi", "y")
ALL = DP + FEAT
EPS = 1e-05
FWD = [(i, (i + 1) % 4) for i in range(4)]
BWD = [(i, (i + 3) % 4) for i in range(4)]
SWAP = [(0, 1), (1, 0)]
OWN, CORE, CHIP = 20, 160, 320


def sibling(a):
    return lax.ppermute(a, "core", SWAP)


def across(a):
    return lax.ppermute(a, "zlo", SWAP)


def right(a):
    return lax.ppermute(a, "x", FWD)


def left(a):
    return lax.ppermute(a, "x", BWD)


def exchange(a, axes):
    return lax.all_to_all(a, axes, 0, 0, tiled=True)


def together(*arrays):
    return lax.optimization_barrier(arrays)


def dot(a, b, dims):
    return lax.dot_general(a, b, (dims, ((), ())), preferred_element_type=F32)


def shape(dims, dtype=BF):
    return jax.ShapeDtypeStruct(dims, dtype)


def call(body, outs, *args, scratch=(), scalars=0, remote_in=0, remote_out=0, room=16):
    whole = pl.BlockSpec(memory_space=pltpu.VMEM)
    small = pl.BlockSpec(memory_space=pltpu.SMEM)
    there = pl.BlockSpec(memory_space=pltpu.HBM)
    return pl.pallas_call(
        body,
        out_shape=outs,
        in_specs=[small] * scalars
        + [whole] * (len(args) - scalars - remote_in)
        + [there] * remote_in,
        out_specs=[there] * remote_out + [whole] * (len(outs) - remote_out),
        scratch_shapes=list(scratch),
        compiler_params=pltpu.CompilerParams(vmem_limit_bytes=room * 1024 * 1024),
    )(*args)


def one_where(dims, test):
    rows = lax.broadcasted_iota(jnp.int32, dims, 0)
    cols = lax.broadcasted_iota(jnp.int32, dims, 1)
    return test(rows, cols).astype(F32).astype(BF)


def many(start, size):
    return pl.ds(pl.multiple_of(start, size), size)


def halves(core, width):
    return many(core * width, width), many((1 - core) * width, width)


def chip_rows(core):
    return one_where((256, 128), lambda r, c: r == (c % 16) * 16 + core * 8 + c // 16)


def send_kernel(place, up, down, sent, sems):
    unused, other = halves(place[0], 512)
    low, high = many((1 - place[0]) * 512, 256), many((1 - place[0]) * 512 + 256, 256)
    copies = [
        pltpu.make_async_copy(up.at[:, other], sent.at[pl.ds(0, 128)], sems.at[0]),
        pltpu.make_async_copy(
            down.at[low], sent.at[pl.ds(128, 256), pl.ds(0, 256)], sems.at[1]
        ),
        pltpu.make_async_copy(
            down.at[high], sent.at[pl.ds(128, 256), pl.ds(256, 256)], sems.at[2]
        ),
    ]
    for copy in copies:
        copy.start()
    for copy in copies:
        copy.wait()


def message_kernel(place, proj, mix, emb, message, sems):
    copy = pltpu.make_async_copy(emb, message.at[:, pl.ds(0, 320)], sems.at[0])
    copy.start()
    here = one_where((16, 128), lambda n, lane: lane == place[3] * 16 + n)
    proj_rows = dot(proj[...], here, ((0,), (0,))).astype(BF)
    shift = one_where((16, 12), lambda u, c: u == c + 4)
    mix_rows = dot(shift, mix[...], ((1,), (0,))).astype(BF)
    for group in range(8):
        message[group, 320:336] = proj_rows
        message[group, 336:352] = mix_rows
    copy.wait()


def piece_kernel(place, got, up, down, out, token, piece, mine_up, mine_down, sems):
    core = place[0]
    token[...] = got[:16, :128]
    mine, unused = halves(core, 512)
    copies = [
        pltpu.make_async_copy(up.at[:, mine], mine_up, sems.at[0]),
        pltpu.make_async_copy(down.at[mine], mine_down, sems.at[1]),
    ]
    for copy in copies:
        copy.start()
    mine_at, other_at = halves(core, 256)
    piece[16:32, :, other_at] = got[128:, :256].reshape(16, 16, 256)
    piece[32:, :, other_at] = got[128:, 256:].reshape(16, 16, 256)
    rows = dot(chip_rows(1 - core), got[:128], ((1,), (0,)))
    copies[0].wait()
    rows += dot(chip_rows(core), mine_up[...], ((1,), (0,)))
    piece[:16] = rows.astype(BF).reshape(16, 16, 512)
    copies[1].wait()
    piece[16:, :, mine_at] = mine_down[...].reshape(32, 16, 256)
    copy = pltpu.make_async_copy(piece, out, sems.at[2])
    copy.start()
    copy.wait()


def total_of(refs):
    total = refs[0][...].astype(F32)
    for ref in refs[1:]:
        total += ref[...].astype(F32)
    return total.astype(BF)


def add_kernel(parts, *refs):
    *terms, out, held, total, sems, out_sems = refs
    sends, taken = [], {}
    for step in range(0, 48, 12):
        taken[step] = []
        for i, (start, first, count) in enumerate(parts):
            if first <= step < first + count:
                there = terms[i].at[pl.ds(start + step - first, 12)]
                sem = sems.at[step // 12 * len(parts) + i]
                copy = pltpu.make_async_copy(there, held.at[i, pl.ds(step, 12)], sem)
                copy.start()
                taken[step].append((i, copy))
    for step in range(0, 48, 12):
        at = slice(step, step + 12)
        part = jnp.zeros((12, 16, 512), F32)
        for i, copy in taken[step]:
            copy.wait()
            part += held[i, at].astype(F32)
        total[at] = part.astype(BF)
        if out is not None:
            at = pl.ds(step, 12)
            sem = out_sems.at[step // 12]
            sends.append(pltpu.make_async_copy(total.at[at], out.at[at], sem))
            sends[-1].start()
    for copy in sends:
        copy.wait()


def add_scratch(terms):
    return [
        pltpu.VMEM((terms, 48, 16, 512), BF),
        pltpu.VMEM((48, 16, 512), BF),
        pltpu.SemaphoreType.DMA((4 * terms,)),
        pltpu.SemaphoreType.DMA((4,)),
    ]


def add(*parts):
    parts = [(array, start, *(where or (0, 48))) for array, start, *where in parts]
    terms = [array for array, *unused in parts]
    return call(
        functools.partial(add_kernel, [where for unused, *where in parts]),
        [shape((48, 16, 512))],
        *terms,
        scratch=add_scratch(len(terms)),
        remote_in=len(terms),
        remote_out=1,
        room=60,
    )[0]


def sum_kernel(*refs):
    refs[-1][...] = total_of(refs[:-1])


def join_kernel(own, got, layer, out):
    out[:, :16] = total_of((own, got))
    out[:, 16:] = layer[...]


def split_kernel(place, late, one, two, three, up_kept, down_kept, sent, held, total, *sems):
    core = place[0]
    whole = [(start, 0, 48) for start in (0, 0, 0, 0)]
    add_kernel(whole, late, one, two, three, None, held, total, *sems)
    total = total[...]
    up, down = total[:16].reshape(256, 512), total[16:].reshape(512, 512)
    up_kept[...] = dot(chip_rows(core), up, ((0,), (0,))).astype(BF)
    sent[:128] = dot(chip_rows(1 - core), up, ((0,), (0,))).astype(BF)
    first, second = down[:, :256], down[:, 256:]
    down_kept[...] = jnp.where(core == 0, first, second)
    other = jnp.where(core == 0, second, first)
    sent[128:, :256] = other[:256]
    sent[128:, 256:] = other[256:]


def finish_kernel(place, up_kept, down_kept, got, last, up, down, gain, mix, proj):
    mine, other = halves(place[0], 512)
    up[:, mine] = up_kept[...]
    up[:, other] = got[:128]
    down[mine, :] = down_kept[...]
    down[other, :] = jnp.concatenate([got[128:, :256], got[128:, 256:]], 0)
    total = jnp.sum(last[...].astype(F32), axis=0)
    gain[...] = total[2:3]
    mix[...] = total[4:]
    token = lax.broadcasted_iota(jnp.int32, (16, 128), 0)
    lane = lax.broadcasted_iota(jnp.int32, (16, 128), 1)
    rows = jnp.where(token < 8, total[0:1], total[1:2])
    rows = jnp.where(token % 8 == lane // 16, rows, 0.0)
    pick = one_where((128, 16), lambda r, k: r % 16 == k).astype(F32)
    proj[...] = jnp.dot(
        rows, pick, precision=lax.Precision.HIGHEST, preferred_element_type=F32
    )


def unpack(ref, width, start, size):
    quarter = start // (width // 4)
    tail = width + start - quarter * (width // 4)
    rest = ref[:, :16, tail : tail + size].astype(F32)
    rest = [rest[f, 4 * quarter : 4 * quarter + 4] for f in range(8)]
    rest = jnp.concatenate(rest, 0).astype(BF)
    return [ref[:, :16, start : start + size].reshape(128, size), rest]


def pack(part, ref, tails, width, start, size):
    quarter = start // (width // 4)
    tail = start - quarter * (width // 4)
    ref[:, :, start : start + size] = part[:128].astype(BF).reshape(8, 16, size)
    for f in range(8):
        row = 16 * f + 4 * quarter
        tails[row : row + 4, tail : tail + size] = part[128 + 4 * f : 132 + 4 * f]
    if quarter == 3:
        rest = tails[:, tail : tail + size].astype(BF)
        ref[:, :, width + tail : width + tail + size] = rest.reshape(8, 16, size)


def chip_of(place, r):
    return jnp.bitwise_xor(place[1], r // 4) * 4 + lax.rem(place[2] + r % 4, 4)


def fetch(place, pieces, first_held, second_held, sems):
    first, second = [], []
    for r, piece in enumerate(pieces):
        at = first_held.at[:, many(chip_of(place, r) * 16, 16)]
        first.append(pltpu.make_async_copy(piece.at[pl.ds(0, 16)], at, sems.at[r]))
        copy = pltpu.make_async_copy(piece.at[pl.ds(16, 32)], second_held.at[r], sems.at[8 + r])
        second.append(copy)
    return first, second


def features_kernel(message, payload, normal, rstds, tails):
    proj_w = message[0, 320:336].astype(F32)
    for f in range(1, 8):
        proj_w += message[f, 320:336].astype(F32)
    proj_w = proj_w.astype(BF)

    def sample(b, carry):
        tokens = message[:, many(b * 16, 16)].reshape(128, 128)
        proj = dot(proj_w, tokens, ((1,), (0,))).astype(BF)
        inter = dot(proj, tokens, ((1,), (1,)))
        cent = inter - jnp.sum(inter, keepdims=True) * (1.0 / 2048)
        rstd = lax.rsqrt(jnp.sum(cent * cent, keepdims=True) * (1.0 / 2048) + EPS)
        normal[b] = cent * rstd
        rstds[b] = jnp.broadcast_to(rstd, (16, 128))
        return carry

    lax.fori_loop(0, OWN, sample, 0, unroll=5)
    for k in range(16):
        block = normal[:, k, :]
        quarter, tail = k // 4 * 4, k % 4 * 128
        tails[quarter : quarter + 4, tail : tail + 128] = block[16:]
        block = block[:16].astype(BF)
        for f in range(8):
            payload[f, :, 128 * k : 128 * k + 128] = block
    block = tails[...].astype(BF)
    for f in range(8):
        payload[f, :, 2048:] = block


def forward_kernel(place, own, sib, *refs):
    hidden, pre, rows, held, held_down, fmb_own, fmb_sib, tail_own, tail_sib, sems = refs[8:]
    first, second = fetch(place, refs[:8], held, held_down, sems)
    for copy in first + second:
        copy.start()
    for j in range(8):
        part = unpack(own, 2048, 256 * j, 256) + unpack(sib, 2048, 256 * j, 256)
        rows[:, 256 * j : 256 * j + 256] = jnp.concatenate(part, 0)
    for copy in first:
        copy.wait()
    total = dot(rows[...], held[...].reshape(2048, 512), ((1,), (0,)))
    pre[...] = total
    act = (total / (1.0 + jnp.exp(-total))).astype(BF)
    hidden[...] = act
    for copy in second:
        copy.wait()
    for r in range(8):
        part = dot(act, held_down[r].reshape(512, 512), ((1,), (0,)))
        pack(part[:CORE], fmb_own, tail_own, 4096, 512 * r, 512)
        pack(part[CORE:], fmb_sib, tail_sib, 4096, 512 * r, 512)


def backward_kernel(place, d_own, d_sib, rows, hidden, pre, held, held_down, *refs):
    far1_low, far1_high, far0_low, far0_high, late, dn_own, dn_sib = refs[:7]
    d_rows, made, made_down, tail_own, tail_sib, out_sems = refs[7:]
    halves_of = {2: (far0_low, far0_high), 6: (far1_low, far1_high)}
    starts = {0: 0, 4: 48, 5: 96, 7: 144, 1: 192, 3: 240}
    total = jnp.zeros((CHIP, 512), F32)
    for r in range(8):
        part = unpack(d_own, 4096, 512 * r, 512) + unpack(d_sib, 4096, 512 * r, 512)
        part = jnp.concatenate(part, 0)
        d_rows[:, 512 * r : 512 * r + 512] = part
        total += dot(part, held_down[r].reshape(512, 512), ((1,), (1,)))
    sends = []

    def send(source, there, sem):
        sends.append(pltpu.make_async_copy(source, there, out_sems.at[sem]))
        sends[-1].start()

    act = hidden[...].T
    for r in (6, 7, 2, 5, 4, 1, 3, 0):
        part = dot(act, d_rows[:, 512 * r : 512 * r + 512], ((1,), (0,)))
        made_down[r] = part.astype(BF).reshape(32, 16, 512)
        if r in halves_of:
            low, high = halves_of[r]
            send(made_down.at[r, pl.ds(0, 8)], low.at[pl.ds(16, 8)], 8 + r)
            send(made_down.at[r, pl.ds(8, 24)], high, 16 + r // 4)
        else:
            send(made_down.at[r], late.at[pl.ds(starts[r] + 16, 32)], 8 + r)
    sig = 1.0 / (1.0 + jnp.exp(-pre[...]))
    d_pre = (total * (sig * (1.0 + pre[...] * (1.0 - sig)))).astype(BF)
    for j in range(8):
        part = dot(rows[:, 256 * j : 256 * j + 256], d_pre, ((0,), (0,)))
        made[2 * j : 2 * j + 2] = part.astype(BF).reshape(2, 128, 512)
    for r in range(8):
        there = halves_of[r][0] if r in halves_of else late.at[pl.ds(starts[r], 48)]
        here = made.at[:, many(chip_of(place, r) * 16, 16)]
        send(here, there.at[pl.ds(0, 16)], r)
    for j in range(8):
        part = dot(d_pre, held[2 * j : 2 * j + 2].reshape(256, 512), ((1,), (1,)))
        pack(part[:CORE], dn_own, tail_own, 2048, 256 * j, 256)
        pack(part[CORE:], dn_sib, tail_sib, 2048, 256 * j, 256)
    for copy in sends:
        copy.wait()


def norm_kernel(
    place, parts, message, cot, gain, layer, d_fmb, mix_part, gain_part, fm, grad, tails
):
    def added(cols):
        total = parts[0, :, cols].astype(F32)
        for f in range(1, 8):
            total += parts[f, :, cols].astype(F32)
        return total

    fm[...] = jnp.zeros_like(fm)
    tails[...] = added(slice(4096, 5120))
    for r in range(8):
        main = added(slice(512 * r, 512 * r + 512))
        quarter, tail = r // 2 * 4, r % 2 * 512
        for u in range(4):
            at = slice(128 * u, 128 * u + 128)
            fm[:16, chip_of(place, r), u, :] = main[:, at]
            at = slice(tail + 128 * u, tail + 128 * u + 128)
            fm[16:, chip_of(place, r), u, :] = tails[quarter : quarter + 4, at]
    mix_part[...] = jnp.zeros_like(mix_part)
    gain_part[...] = jnp.zeros_like(gain_part)
    scale = gain[...]
    mixing = message[:, 336:352].reshape(128, 128)

    def mean(a):
        return jnp.sum(a, axis=1, keepdims=True) * (1.0 / 128)

    def sample(b, carry):
        at = many(b * 16, 16)
        tokens = message[:, at].reshape(128, 128)
        cotan = cot[:, at].reshape(128, 128).astype(F32)
        lcb = dot(mixing, tokens, ((1,), (0,)))
        summed = lcb + fm[b].reshape(128, 128) + tokens.astype(F32)
        cent = summed - mean(summed)
        rstd = lax.rsqrt(mean(cent * cent) + EPS)
        normal = cent * rstd
        layer[:, :, many(b * 128, 128)] = (normal * scale).astype(BF).reshape(8, 16, 128)
        gain_part[...] += jnp.sum((cotan * normal).reshape(16, 8, 128), axis=0)
        dnorm = cotan * scale
        dsum = rstd * (dnorm - mean(dnorm) - normal * mean(dnorm * normal))
        grad[b] = dsum.reshape(8, 16, 128)
        mix_part[...] += dot(dsum.astype(BF), tokens, ((1,), (1,)))
        return carry

    lax.fori_loop(0, OWN, sample, 0, unroll=5)
    for r in range(8):
        quarter, tail = r // 2 * 4, r % 2 * 512
        for u in range(4):
            block = grad[:, chip_of(place, r), u, :]
            at = slice(tail + 128 * u, tail + 128 * u + 128)
            tails[quarter : quarter + 4, at] = block[16:]
            block = block[:16].astype(BF)
            for f in range(8):
                d_fmb[f, :, 512 * r + 128 * u : 512 * r + 128 * u + 128] = block
    block = tails[...].astype(BF)
    for f in range(8):
        d_fmb[f, :, 4096:] = block


def last_kernel(back, normal, rstds, message, mix_part, gain_part, last, grad, proj_part):
    total = back[0, :16].astype(F32)
    for f in range(1, 8):
        total += back[f, :16].astype(F32)
    for k in range(16):
        quarter, tail = k // 4 * 4, 2048 + k % 4 * 128
        grad[:16, k, :] = total[:, 128 * k : 128 * k + 128]
        grad[16:, k, :] = total[quarter : quarter + 4, tail : tail + 128]
    proj_part[...] = jnp.zeros_like(proj_part)

    def sample(b, carry):
        tokens = message[:, many(b * 16, 16)].reshape(128, 128)
        d_normed, norm = grad[b], normal[b]
        first = jnp.sum(d_normed, keepdims=True) * (1.0 / 2048)
        second = jnp.sum(d_normed * norm, keepdims=True) * (1.0 / 2048)
        d_inter = rstds[b] * (d_normed - first - norm * second)
        d_proj = dot(d_inter.astype(BF), tokens, ((1,), (0,)))
        proj_part[...] += dot(d_proj.astype(BF), tokens, ((1,), (1,)))
        return carry

    lax.fori_loop(0, OWN, sample, 0, unroll=5)
    repeat = one_where((16, 128), lambda k, lane: lane % 16 == k)
    spread = dot(proj_part[...].astype(BF), repeat, ((0,), (0,)))
    token = lax.broadcasted_iota(jnp.int32, (128, 128), 0)
    lane = lax.broadcasted_iota(jnp.int32, (128, 128), 1)
    spread = jnp.where(token % 8 == lane // 16, spread, 0.0).astype(BF)
    collect = one_where(
        (128, 128), lambda r, n: (r % 16 < 2) & (n // 8 == (r // 16) * 2 + r % 16)
    )
    rows = dot(collect, spread, ((1,), (0,)))
    gain = jnp.sum(gain_part[...], axis=0, keepdims=True)
    rows += jnp.where(token % 16 == 2, jnp.broadcast_to(gain, (128, 128)), 0.0)
    rows += jnp.where(token % 16 >= 4, mix_part[...], 0.0)
    rows = rows.astype(BF).reshape(8, 16, 128)
    for d in range(16):
        last[8 * d : 8 * d + 8] = rows


def unfold_kernel(back, layer):
    for b in range(OWN):
        layer[:, b] = back[:, 16:, 128 * b : 128 * b + 128]


def per_device(embeddings, proj_weight, up_weight, down_weight, mix_weight, out_gain, cotangent):
    place = jnp.stack(
        [lax.axis_index(axis) for axis in ("core", "zlo", "x")]
        + [lax.axis_index("zhi") * 4 + lax.axis_index("y")]
    ).astype(jnp.int32)
    (sent,) = call(
        send_kernel,
        [shape((384, 512))],
        place,
        up_weight,
        down_weight,
        scratch=[pltpu.SemaphoreType.DMA((3,))],
        scalars=1,
        remote_in=2,
    )
    mine, token = call(
        piece_kernel,
        [shape((48, 16, 512)), shape((16, 128))],
        place,
        sibling(sent),
        up_weight,
        down_weight,
        scratch=[
            pltpu.VMEM((48, 16, 512), BF),
            pltpu.VMEM((128, 512), BF),
            pltpu.VMEM((512, 256), BF),
            pltpu.SemaphoreType.DMA((3,)),
        ],
        scalars=1,
        remote_in=2,
        remote_out=1,
    )
    other = across(mine)
    near_left, near_right = right(mine), left(mine)
    (message,) = call(
        message_kernel,
        [shape((8, 352, 128))],
        place,
        proj_weight,
        mix_weight.T,
        embeddings.reshape(8, 320, 128),
        scratch=[pltpu.SemaphoreType.DMA((1,))],
        scalars=1,
        remote_in=1,
    )
    message, token = together(message, sibling(token))
    message = exchange(message, FEAT)
    message, near_left, near_right, other = together(message, near_left, near_right, other)
    other_left, other_right = right(other), left(other)

    payload, normal1, rstd1 = call(
        features_kernel,
        [shape((8, 16, 2560)), shape((OWN, 16, 128), F32), shape((OWN, 16, 128), F32)],
        message,
        scratch=[pltpu.VMEM((16, 512), F32)],
    )
    payload, cotangent = together(payload, cotangent)
    cotan = exchange(cotangent.reshape(8, 320, 128), FEAT)
    payload, cotan, token, near_left, other_left, other_right = together(
        payload, cotan, token, near_left, other_left, other_right
    )
    far, other_far = right(near_left), left(other_right)
    payload, token = together(payload, sibling(token))
    normed = exchange(payload, FEAT)
    normed, far, other_far = together(normed, far, other_far)
    weights = [mine, near_right, far, near_left, other, other_right, other_far, other_left]
    hidden, pre, rows, first, second, fmb_own, fmb_sib = call(
        forward_kernel,
        [
            shape((CHIP, 512)),
            shape((CHIP, 512), F32),
            shape((CHIP, 2048)),
            shape((16, 128, 512)),
            shape((8, 32, 16, 512)),
            shape((8, 16, 5120)),
            shape((8, 16, 5120)),
        ],
        place,
        normed,
        sibling(normed),
        *weights,
        scratch=[
            pltpu.VMEM((128, 1024), F32),
            pltpu.VMEM((128, 1024), F32),
            pltpu.SemaphoreType.DMA((16,)),
        ],
        scalars=1,
        remote_in=8,
    )
    (fmb,) = call(sum_kernel, [shape((8, 16, 5120))], fmb_own, sibling(fmb_sib))
    fmb = exchange(fmb, FEAT)

    layer_out, d_fmb, mix_part, gain_part = call(
        norm_kernel,
        [
            shape((8, 16, 2560)),
            shape((8, 16, 5120)),
            shape((128, 128), F32),
            shape((8, 128), F32),
        ],
        place,
        fmb,
        message,
        cotan,
        out_gain.reshape(1, 128),
        scratch=[
            pltpu.VMEM((OWN, 8, 16, 128), F32),
            pltpu.VMEM((OWN, 8, 16, 128), F32),
            pltpu.VMEM((16, 1024), F32),
        ],
        scalars=1,
    )

    d_fmb = exchange(d_fmb, FEAT)
    far1_low, far1_high, far0_low, far0_high, late, dn_own, dn_sib = call(
        backward_kernel,
        [shape((24, 16, 512))] * 4 + [shape((288, 16, 512))] + [shape((8, 16, 2560))] * 2,
        place,
        d_fmb,
        sibling(d_fmb),
        rows,
        hidden,
        pre,
        first,
        second,
        scratch=[
            pltpu.VMEM((CHIP, 4096), BF),
            pltpu.VMEM((16, 128, 512), BF),
            pltpu.VMEM((8, 32, 16, 512), BF),
            pltpu.VMEM((128, 512), F32),
            pltpu.VMEM((128, 512), F32),
            pltpu.SemaphoreType.DMA((18,)),
        ],
        scalars=1,
        remote_out=5,
        room=24,
    )

    low1, high1 = right(far1_low), left(far1_high)
    low0, high0 = right(far0_low), left(far0_high)
    (back,) = call(join_kernel, [shape((8, 32, 2560))], dn_own, sibling(dn_sib), layer_out)
    back = exchange(back, FEAT)
    plus1 = add((late, 96), (low1, 0, 0, 24))
    minus1 = add((late, 144), (high1, 0, 24, 24))
    plus1, minus1, low0, high0 = together(plus1, minus1, low0, high0)
    from_left1, from_right1 = right(plus1), left(minus1)
    plus0 = add((late, 192), (low0, 0, 0, 24))
    minus0 = add((late, 240), (high0, 0, 24, 24))
    back, plus0, minus0 = together(back, plus0, minus0)
    from_left0, from_right0 = right(plus0), left(minus0)
    (last,) = call(
        last_kernel,
        [shape((128, 16, 128))],
        back,
        normal1,
        rstd1,
        message,
        mix_part,
        gain_part,
        scratch=[pltpu.VMEM((OWN, 16, 128), F32), pltpu.VMEM((16, 128), F32)],
    )
    from_left1, from_right1, last = together(from_left1, from_right1, last)
    over = add((late, 48), (from_left1, 0), (from_right1, 0))
    over, last = together(over, last)
    other = across(over)
    last, other = together(exchange(last, ALL), other)
    up_kept, down_kept, sent = call(
        split_kernel,
        [shape((128, 512)), shape((512, 256)), shape((384, 512))],
        place,
        late,
        from_left0,
        from_right0,
        other,
        scratch=add_scratch(4),
        scalars=1,
        remote_in=4,
        room=60,
    )
    up_grad, down_grad, gain_grad, mix_grad, proj_grad = call(
        finish_kernel,
        [
            shape((128, 1024)),
            shape((1024, 256)),
            shape((1, 128), F32),
            shape((12, 128), F32),
            shape((16, 16), F32),
        ],
        place,
        up_kept,
        down_kept,
        sibling(sent),
        last,
        scalars=1,
    )
    (layer_out,) = call(unfold_kernel, [shape((8, OWN, 16, 128))], back)
    gain_grad, mix_grad = gain_grad.reshape(128), mix_grad.T
    layer_out = layer_out.reshape(160, 16, 128)
    return (layer_out, gain_grad, mix_grad, up_grad, down_grad, proj_grad)


def solution(mesh):
    grid = Mesh(mesh.devices.reshape(2, 4, 2, 2, 4), ALL)
    placed = (
        P(DP, FEAT, None),
        P(FEAT, None),
        P(DP, FEAT),
        P(FEAT, DP),
        P(None, FEAT),
        P(),
        P(DP, FEAT, None),
    )
    return jax.shard_map(
        per_device,
        mesh=grid,
        in_specs=placed,
        out_specs=(
            P(DP, FEAT, None),
            P(),
            P(None, FEAT),
            P(DP, FEAT),
            P(FEAT, DP),
            P(FEAT, None),
        ),
        check_vma=False,
    )
```

```python
import functools

import jax
import jax.numpy as jnp
from jax import lax
from jax.experimental import pallas as pl
from jax.experimental.pallas import tpu as pltpu
from jax.sharding import Mesh, PartitionSpec as P

BF = jnp.bfloat16
F32 = jnp.float32
DP = ("zlo", "x", "core")
FEAT = ("zhi", "y")
ALL = DP + FEAT
EPS = 1e-05
FWD = [(i, (i + 1) % 4) for i in range(4)]
BWD = [(i, (i + 3) % 4) for i in range(4)]
SWAP = [(0, 1), (1, 0)]
OWN, CORE, CHIP = 20, 160, 320


def sibling(a):
    return lax.ppermute(a, "core", SWAP)


def across(a):
    return lax.ppermute(a, "zlo", SWAP)


def right(a):
    return lax.ppermute(a, "x", FWD)


def left(a):
    return lax.ppermute(a, "x", BWD)


def exchange(a, axes):
    return lax.all_to_all(a, axes, 0, 0, tiled=True)


def together(*arrays):
    return lax.optimization_barrier(arrays)


def dot(a, b, dims):
    return lax.dot_general(a, b, (dims, ((), ())), preferred_element_type=F32)


def shape(dims, dtype=BF):
    return jax.ShapeDtypeStruct(dims, dtype)


def call(body, outs, *args, scratch=(), scalars=0, remote_in=0, remote_out=0, room=16):
    whole = pl.BlockSpec(memory_space=pltpu.VMEM)
    small = pl.BlockSpec(memory_space=pltpu.SMEM)
    there = pl.BlockSpec(memory_space=pltpu.HBM)
    return pl.pallas_call(
        body,
        out_shape=outs,
        in_specs=[small] * scalars
        + [whole] * (len(args) - scalars - remote_in)
        + [there] * remote_in,
        out_specs=[there] * remote_out + [whole] * (len(outs) - remote_out),
        scratch_shapes=list(scratch),
        compiler_params=pltpu.CompilerParams(vmem_limit_bytes=room * 1024 * 1024),
    )(*args)


def one_where(dims, test):
    rows = lax.broadcasted_iota(jnp.int32, dims, 0)
    cols = lax.broadcasted_iota(jnp.int32, dims, 1)
    return test(rows, cols).astype(F32).astype(BF)


def many(start, size):
    return pl.ds(pl.multiple_of(start, size), size)


def halves(core, width):
    return many(core * width, width), many((1 - core) * width, width)


def chip_rows(core):
    return one_where((256, 128), lambda r, c: r == (c % 16) * 16 + core * 8 + c // 16)


def send_kernel(place, up, down, sent, sems):
    unused, other = halves(place[0], 512)
    low, high = many((1 - place[0]) * 512, 256), many((1 - place[0]) * 512 + 256, 256)
    copies = [
        pltpu.make_async_copy(up.at[:, other], sent.at[pl.ds(0, 128)], sems.at[0]),
        pltpu.make_async_copy(
            down.at[low], sent.at[pl.ds(128, 256), pl.ds(0, 256)], sems.at[1]
        ),
        pltpu.make_async_copy(
            down.at[high], sent.at[pl.ds(128, 256), pl.ds(256, 256)], sems.at[2]
        ),
    ]
    for copy in copies:
        copy.start()
    for copy in copies:
        copy.wait()


def message_kernel(place, proj, mix, emb, message, sems):
    copy = pltpu.make_async_copy(emb, message.at[:, pl.ds(0, 320)], sems.at[0])
    copy.start()
    here = one_where((16, 128), lambda n, lane: lane == place[3] * 16 + n)
    proj_rows = dot(proj[...], here, ((0,), (0,))).astype(BF)
    shift = one_where((16, 12), lambda u, c: u == c + 4)
    mix_rows = dot(shift, mix[...], ((1,), (0,))).astype(BF)
    for group in range(8):
        message[group, 320:336] = proj_rows
        message[group, 336:352] = mix_rows
    copy.wait()


def piece_kernel(place, got, up, down, out, token, piece, mine_up, mine_down, sems):
    core = place[0]
    token[...] = got[:16, :128]
    mine, unused = halves(core, 512)
    copies = [
        pltpu.make_async_copy(up.at[:, mine], mine_up, sems.at[0]),
        pltpu.make_async_copy(down.at[mine], mine_down, sems.at[1]),
    ]
    for copy in copies:
        copy.start()
    mine_at, other_at = halves(core, 256)
    piece[16:32, :, other_at] = got[128:, :256].reshape(16, 16, 256)
    piece[32:, :, other_at] = got[128:, 256:].reshape(16, 16, 256)
    rows = dot(chip_rows(1 - core), got[:128], ((1,), (0,)))
    copies[0].wait()
    rows += dot(chip_rows(core), mine_up[...], ((1,), (0,)))
    piece[:16] = rows.astype(BF).reshape(16, 16, 512)
    copies[1].wait()
    piece[16:, :, mine_at] = mine_down[...].reshape(32, 16, 256)
    copy = pltpu.make_async_copy(piece, out, sems.at[2])
    copy.start()
    copy.wait()


def total_of(refs):
    total = refs[0][...].astype(F32)
    for ref in refs[1:]:
        total += ref[...].astype(F32)
    return total.astype(BF)


def add_kernel(parts, *refs):
    *terms, out, held, total, sems, out_sems = refs
    sends, taken = [], {}
    for step in range(0, 48, 12):
        taken[step] = []
        for i, (start, first, count) in enumerate(parts):
            if first <= step < first + count:
                there = terms[i].at[pl.ds(start + step - first, 12)]
                sem = sems.at[step // 12 * len(parts) + i]
                copy = pltpu.make_async_copy(there, held.at[i, pl.ds(step, 12)], sem)
                copy.start()
                taken[step].append((i, copy))
    for step in range(0, 48, 12):
        at = slice(step, step + 12)
        part = jnp.zeros((12, 16, 512), F32)
        for i, copy in taken[step]:
            copy.wait()
            part += held[i, at].astype(F32)
        total[at] = part.astype(BF)
        if out is not None:
            at = pl.ds(step, 12)
            sem = out_sems.at[step // 12]
            sends.append(pltpu.make_async_copy(total.at[at], out.at[at], sem))
            sends[-1].start()
    for copy in sends:
        copy.wait()


def add_scratch(terms):
    return [
        pltpu.VMEM((terms, 48, 16, 512), BF),
        pltpu.VMEM((48, 16, 512), BF),
        pltpu.SemaphoreType.DMA((4 * terms,)),
        pltpu.SemaphoreType.DMA((4,)),
    ]


def add(*parts):
    parts = [(array, start, *(where or (0, 48))) for array, start, *where in parts]
    terms = [array for array, *unused in parts]
    return call(
        functools.partial(add_kernel, [where for unused, *where in parts]),
        [shape((48, 16, 512))],
        *terms,
        scratch=add_scratch(len(terms)),
        remote_in=len(terms),
        remote_out=1,
        room=60,
    )[0]


def sum_kernel(*refs):
    refs[-1][...] = total_of(refs[:-1])


def join_kernel(own, got, layer, out):
    out[:, :16] = total_of((own, got))
    out[:, 16:] = layer[...]


def split_kernel(place, one, two, up_kept, down_kept, sent, held, total, *sems):
    core = place[0]
    add_kernel([(0, 0, 48)] * 2, one, two, None, held, total, *sems)
    total = total[...]
    up, down = total[:16].reshape(256, 512), total[16:].reshape(512, 512)
    up_kept[...] = dot(chip_rows(core), up, ((0,), (0,))).astype(BF)
    sent[:128] = dot(chip_rows(1 - core), up, ((0,), (0,))).astype(BF)
    first, second = down[:, :256], down[:, 256:]
    down_kept[...] = jnp.where(core == 0, first, second)
    other = jnp.where(core == 0, second, first)
    sent[128:, :256] = other[:256]
    sent[128:, 256:] = other[256:]


def finish_kernel(place, up_kept, down_kept, got, last, up, down, gain, mix, proj):
    mine, other = halves(place[0], 512)
    up[:, mine] = up_kept[...]
    up[:, other] = got[:128]
    down[mine, :] = down_kept[...]
    down[other, :] = jnp.concatenate([got[128:, :256], got[128:, 256:]], 0)
    total = jnp.sum(last[...].astype(F32), axis=0)
    gain[...] = total[2:3]
    mix[...] = total[4:]
    token = lax.broadcasted_iota(jnp.int32, (16, 128), 0)
    lane = lax.broadcasted_iota(jnp.int32, (16, 128), 1)
    rows = jnp.where(token < 8, total[0:1], total[1:2])
    rows = jnp.where(token % 8 == lane // 16, rows, 0.0)
    pick = one_where((128, 16), lambda r, k: r % 16 == k).astype(F32)
    proj[...] = jnp.dot(
        rows, pick, precision=lax.Precision.HIGHEST, preferred_element_type=F32
    )


def unpack(ref, width, start, size):
    quarter = start // (width // 4)
    tail = width + start - quarter * (width // 4)
    rest = ref[:, :16, tail : tail + size].astype(F32)
    rest = [rest[f, 4 * quarter : 4 * quarter + 4] for f in range(8)]
    rest = jnp.concatenate(rest, 0).astype(BF)
    return [ref[:, :16, start : start + size].reshape(128, size), rest]


def pack(part, ref, tails, width, start, size):
    quarter = start // (width // 4)
    tail = start - quarter * (width // 4)
    ref[:, :, start : start + size] = part[:128].astype(BF).reshape(8, 16, size)
    for f in range(8):
        row = 16 * f + 4 * quarter
        tails[row : row + 4, tail : tail + size] = part[128 + 4 * f : 132 + 4 * f]
    if quarter == 3:
        rest = tails[:, tail : tail + size].astype(BF)
        ref[:, :, width + tail : width + tail + size] = rest.reshape(8, 16, size)


def chip_of(place, r):
    return jnp.bitwise_xor(place[1], r // 4) * 4 + lax.rem(place[2] + r % 4, 4)


def fetch(place, pieces, first_held, second_held, sems):
    first, second = [], []
    for r, piece in enumerate(pieces):
        at = first_held.at[:, many(chip_of(place, r) * 16, 16)]
        first.append(pltpu.make_async_copy(piece.at[pl.ds(0, 16)], at, sems.at[r]))
        copy = pltpu.make_async_copy(piece.at[pl.ds(16, 32)], second_held.at[r], sems.at[8 + r])
        second.append(copy)
    return first, second


def features_kernel(message, payload, normal, rstds, tails):
    proj_w = message[0, 320:336].astype(F32)
    for f in range(1, 8):
        proj_w += message[f, 320:336].astype(F32)
    proj_w = proj_w.astype(BF)

    def sample(b, carry):
        tokens = message[:, many(b * 16, 16)].reshape(128, 128)
        proj = dot(proj_w, tokens, ((1,), (0,))).astype(BF)
        inter = dot(proj, tokens, ((1,), (1,)))
        cent = inter - jnp.sum(inter, keepdims=True) * (1.0 / 2048)
        rstd = lax.rsqrt(jnp.sum(cent * cent, keepdims=True) * (1.0 / 2048) + EPS)
        normal[b] = cent * rstd
        rstds[b] = jnp.broadcast_to(rstd, (16, 128))
        return carry

    lax.fori_loop(0, OWN, sample, 0, unroll=10)
    for k in range(16):
        block = normal[:, k, :]
        quarter, tail = k // 4 * 4, k % 4 * 128
        tails[quarter : quarter + 4, tail : tail + 128] = block[16:]
        block = block[:16].astype(BF)
        for f in range(8):
            payload[f, :, 128 * k : 128 * k + 128] = block
    block = tails[...].astype(BF)
    for f in range(8):
        payload[f, :, 2048:] = block


def forward_kernel(place, own, sib, *refs):
    hidden, pre, rows, held, held_down, fmb_own, fmb_sib, tail_own, tail_sib, sems = refs[8:]
    first, second = fetch(place, refs[:8], held, held_down, sems)
    for copy in first + second:
        copy.start()
    for j in range(8):
        part = unpack(own, 2048, 256 * j, 256) + unpack(sib, 2048, 256 * j, 256)
        rows[:, 256 * j : 256 * j + 256] = jnp.concatenate(part, 0)
    for copy in first:
        copy.wait()
    total = dot(rows[...], held[...].reshape(2048, 512), ((1,), (0,)))
    pre[...] = total
    act = (total / (1.0 + jnp.exp(-total))).astype(BF)
    hidden[...] = act
    for copy in second:
        copy.wait()
    for r in range(8):
        part = dot(act, held_down[r].reshape(512, 512), ((1,), (0,)))
        pack(part[:CORE], fmb_own, tail_own, 4096, 512 * r, 512)
        pack(part[CORE:], fmb_sib, tail_sib, 4096, 512 * r, 512)


def backward_kernel(place, d_own, d_sib, rows, hidden, pre, held, held_down, *refs):
    far1_low, far1_high, far0_low, far0_high, late, dn_own, dn_sib = refs[:7]
    d_rows, made, made_down, tail_own, tail_sib, out_sems = refs[7:]
    halves_of = {2: (far0_low, far0_high), 6: (far1_low, far1_high)}
    starts = {0: 0, 4: 48, 5: 96, 7: 144, 1: 192, 3: 240}
    total = jnp.zeros((CHIP, 512), F32)
    for r in range(8):
        part = unpack(d_own, 4096, 512 * r, 512) + unpack(d_sib, 4096, 512 * r, 512)
        part = jnp.concatenate(part, 0)
        d_rows[:, 512 * r : 512 * r + 512] = part
        total += dot(part, held_down[r].reshape(512, 512), ((1,), (1,)))
    sends = []

    def send(source, there, sem):
        sends.append(pltpu.make_async_copy(source, there, out_sems.at[sem]))
        sends[-1].start()

    act = hidden[...].T
    for r in (6, 7, 2, 5, 4, 1, 3, 0):
        part = dot(act, d_rows[:, 512 * r : 512 * r + 512], ((1,), (0,)))
        made_down[r] = part.astype(BF).reshape(32, 16, 512)
        if r in halves_of:
            low, high = halves_of[r]
            send(made_down.at[r, pl.ds(0, 8)], low.at[pl.ds(16, 8)], 8 + r)
            send(made_down.at[r, pl.ds(8, 24)], high, 16 + r // 4)
        else:
            send(made_down.at[r], late.at[pl.ds(starts[r] + 16, 32)], 8 + r)
    sig = 1.0 / (1.0 + jnp.exp(-pre[...]))
    d_pre = (total * (sig * (1.0 + pre[...] * (1.0 - sig)))).astype(BF)
    for j in range(8):
        part = dot(rows[:, 256 * j : 256 * j + 256], d_pre, ((0,), (0,)))
        made[2 * j : 2 * j + 2] = part.astype(BF).reshape(2, 128, 512)
    for r in range(8):
        there = halves_of[r][0] if r in halves_of else late.at[pl.ds(starts[r], 48)]
        here = made.at[:, many(chip_of(place, r) * 16, 16)]
        send(here, there.at[pl.ds(0, 16)], r)
    for j in range(8):
        part = dot(d_pre, held[2 * j : 2 * j + 2].reshape(256, 512), ((1,), (1,)))
        pack(part[:CORE], dn_own, tail_own, 2048, 256 * j, 256)
        pack(part[CORE:], dn_sib, tail_sib, 2048, 256 * j, 256)
    for copy in sends:
        copy.wait()


def norm_kernel(
    place, parts, message, cot, gain, layer, d_fmb, mix_part, gain_part, fm, grad, tails
):
    def added(cols):
        total = parts[0, :, cols].astype(F32)
        for f in range(1, 8):
            total += parts[f, :, cols].astype(F32)
        return total

    fm[...] = jnp.zeros_like(fm)
    tails[...] = added(slice(4096, 5120))
    for r in range(8):
        main = added(slice(512 * r, 512 * r + 512))
        quarter, tail = r // 2 * 4, r % 2 * 512
        for u in range(4):
            at = slice(128 * u, 128 * u + 128)
            fm[:16, chip_of(place, r), u, :] = main[:, at]
            at = slice(tail + 128 * u, tail + 128 * u + 128)
            fm[16:, chip_of(place, r), u, :] = tails[quarter : quarter + 4, at]
    mix_part[...] = jnp.zeros_like(mix_part)
    gain_part[...] = jnp.zeros_like(gain_part)
    scale = gain[...]
    mixing = message[:, 336:352].reshape(128, 128)

    def mean(a):
        return jnp.sum(a, axis=1, keepdims=True) * (1.0 / 128)

    def sample(b, carry):
        at = many(b * 16, 16)
        tokens = message[:, at].reshape(128, 128)
        cotan = cot[:, at].reshape(128, 128).astype(F32)
        lcb = dot(mixing, tokens, ((1,), (0,)))
        summed = lcb + fm[b].reshape(128, 128) + tokens.astype(F32)
        cent = summed - mean(summed)
        rstd = lax.rsqrt(mean(cent * cent) + EPS)
        normal = cent * rstd
        layer[:, :, many(b * 128, 128)] = (normal * scale).astype(BF).reshape(8, 16, 128)
        gain_part[...] += jnp.sum((cotan * normal).reshape(16, 8, 128), axis=0)
        dnorm = cotan * scale
        dsum = rstd * (dnorm - mean(dnorm) - normal * mean(dnorm * normal))
        grad[b] = dsum.reshape(8, 16, 128)
        mix_part[...] += dot(dsum.astype(BF), tokens, ((1,), (1,)))
        return carry

    lax.fori_loop(0, OWN, sample, 0, unroll=10)
    for r in range(8):
        quarter, tail = r // 2 * 4, r % 2 * 512
        for u in range(4):
            block = grad[:, chip_of(place, r), u, :]
            at = slice(tail + 128 * u, tail + 128 * u + 128)
            tails[quarter : quarter + 4, at] = block[16:]
            block = block[:16].astype(BF)
            for f in range(8):
                d_fmb[f, :, 512 * r + 128 * u : 512 * r + 128 * u + 128] = block
    block = tails[...].astype(BF)
    for f in range(8):
        d_fmb[f, :, 4096:] = block


def last_kernel(back, normal, rstds, message, mix_part, gain_part, last, grad, proj_part):
    total = back[0, :16].astype(F32)
    for f in range(1, 8):
        total += back[f, :16].astype(F32)
    for k in range(16):
        quarter, tail = k // 4 * 4, 2048 + k % 4 * 128
        grad[:16, k, :] = total[:, 128 * k : 128 * k + 128]
        grad[16:, k, :] = total[quarter : quarter + 4, tail : tail + 128]
    proj_part[...] = jnp.zeros_like(proj_part)

    def sample(b, carry):
        tokens = message[:, many(b * 16, 16)].reshape(128, 128)
        d_normed, norm = grad[b], normal[b]
        first = jnp.sum(d_normed, keepdims=True) * (1.0 / 2048)
        second = jnp.sum(d_normed * norm, keepdims=True) * (1.0 / 2048)
        d_inter = rstds[b] * (d_normed - first - norm * second)
        d_proj = dot(d_inter.astype(BF), tokens, ((1,), (0,)))
        proj_part[...] += dot(d_proj.astype(BF), tokens, ((1,), (1,)))
        return carry

    lax.fori_loop(0, OWN, sample, 0, unroll=10)
    repeat = one_where((16, 128), lambda k, lane: lane % 16 == k)
    spread = dot(proj_part[...].astype(BF), repeat, ((0,), (0,)))
    token = lax.broadcasted_iota(jnp.int32, (128, 128), 0)
    lane = lax.broadcasted_iota(jnp.int32, (128, 128), 1)
    spread = jnp.where(token % 8 == lane // 16, spread, 0.0).astype(BF)
    collect = one_where(
        (128, 128), lambda r, n: (r % 16 < 2) & (n // 8 == (r // 16) * 2 + r % 16)
    )
    rows = dot(collect, spread, ((1,), (0,)))
    gain = jnp.sum(gain_part[...], axis=0, keepdims=True)
    rows += jnp.where(token % 16 == 2, jnp.broadcast_to(gain, (128, 128)), 0.0)
    rows += jnp.where(token % 16 >= 4, mix_part[...], 0.0)
    rows = rows.astype(BF).reshape(8, 16, 128)
    for d in range(16):
        last[8 * d : 8 * d + 8] = rows


def unfold_kernel(back, layer):
    for b in range(OWN):
        layer[:, b] = back[:, 16:, 128 * b : 128 * b + 128]


def per_device(embeddings, proj_weight, up_weight, down_weight, mix_weight, out_gain, cotangent):
    place = jnp.stack(
        [lax.axis_index(axis) for axis in ("core", "zlo", "x")]
        + [lax.axis_index("zhi") * 4 + lax.axis_index("y")]
    ).astype(jnp.int32)
    (sent,) = call(
        send_kernel,
        [shape((384, 512))],
        place,
        up_weight,
        down_weight,
        scratch=[pltpu.SemaphoreType.DMA((3,))],
        scalars=1,
        remote_in=2,
    )
    mine, token = call(
        piece_kernel,
        [shape((48, 16, 512)), shape((16, 128))],
        place,
        sibling(sent),
        up_weight,
        down_weight,
        scratch=[
            pltpu.VMEM((48, 16, 512), BF),
            pltpu.VMEM((128, 512), BF),
            pltpu.VMEM((512, 256), BF),
            pltpu.SemaphoreType.DMA((3,)),
        ],
        scalars=1,
        remote_in=2,
        remote_out=1,
    )
    other = across(mine)
    near_left, near_right = right(mine), left(mine)
    (message,) = call(
        message_kernel,
        [shape((8, 352, 128))],
        place,
        proj_weight,
        mix_weight.T,
        embeddings.reshape(8, 320, 128),
        scratch=[pltpu.SemaphoreType.DMA((1,))],
        scalars=1,
        remote_in=1,
    )
    message, token = together(message, sibling(token))
    message = exchange(message, FEAT)
    message, near_left, near_right, other = together(message, near_left, near_right, other)
    other_left, other_right = right(other), left(other)

    payload, normal1, rstd1 = call(
        features_kernel,
        [shape((8, 16, 2560)), shape((OWN, 16, 128), F32), shape((OWN, 16, 128), F32)],
        message,
        scratch=[pltpu.VMEM((16, 512), F32)],
    )
    payload, cotangent = together(payload, cotangent)
    cotan = exchange(cotangent.reshape(8, 320, 128), FEAT)
    payload, cotan, token, near_left, other_left, other_right = together(
        payload, cotan, token, near_left, other_left, other_right
    )
    far, other_far = right(near_left), left(other_right)
    payload, token = together(payload, sibling(token))
    normed = exchange(payload, FEAT)
    normed, far, other_far = together(normed, far, other_far)
    weights = [mine, near_right, far, near_left, other, other_right, other_far, other_left]
    hidden, pre, rows, first, second, fmb_own, fmb_sib = call(
        forward_kernel,
        [
            shape((CHIP, 512)),
            shape((CHIP, 512), F32),
            shape((CHIP, 2048)),
            shape((16, 128, 512)),
            shape((8, 32, 16, 512)),
            shape((8, 16, 5120)),
            shape((8, 16, 5120)),
        ],
        place,
        normed,
        sibling(normed),
        *weights,
        scratch=[
            pltpu.VMEM((128, 1024), F32),
            pltpu.VMEM((128, 1024), F32),
            pltpu.SemaphoreType.DMA((16,)),
        ],
        scalars=1,
        remote_in=8,
    )
    (fmb,) = call(sum_kernel, [shape((8, 16, 5120))], fmb_own, sibling(fmb_sib))
    fmb = exchange(fmb, FEAT)

    layer_out, d_fmb, mix_part, gain_part = call(
        norm_kernel,
        [
            shape((8, 16, 2560)),
            shape((8, 16, 5120)),
            shape((128, 128), F32),
            shape((8, 128), F32),
        ],
        place,
        fmb,
        message,
        cotan,
        out_gain.reshape(1, 128),
        scratch=[
            pltpu.VMEM((OWN, 8, 16, 128), F32),
            pltpu.VMEM((OWN, 8, 16, 128), F32),
            pltpu.VMEM((16, 1024), F32),
        ],
        scalars=1,
    )

    d_fmb = exchange(d_fmb, FEAT)
    far1_low, far1_high, far0_low, far0_high, late, dn_own, dn_sib = call(
        backward_kernel,
        [shape((24, 16, 512))] * 4 + [shape((288, 16, 512))] + [shape((8, 16, 2560))] * 2,
        place,
        d_fmb,
        sibling(d_fmb),
        rows,
        hidden,
        pre,
        first,
        second,
        scratch=[
            pltpu.VMEM((CHIP, 4096), BF),
            pltpu.VMEM((16, 128, 512), BF),
            pltpu.VMEM((8, 32, 16, 512), BF),
            pltpu.VMEM((128, 512), F32),
            pltpu.VMEM((128, 512), F32),
            pltpu.SemaphoreType.DMA((18,)),
        ],
        scalars=1,
        remote_out=5,
        room=24,
    )

    low1, high1 = right(far1_low), left(far1_high)
    low0, high0 = right(far0_low), left(far0_high)
    (back,) = call(join_kernel, [shape((8, 32, 2560))], dn_own, sibling(dn_sib), layer_out)
    back = exchange(back, FEAT)
    plus1 = add((late, 96), (low1, 0, 0, 24))
    minus1 = add((late, 144), (high1, 0, 24, 24))
    plus1, minus1, low0, high0 = together(plus1, minus1, low0, high0)
    from_left1, from_right1 = right(plus1), left(minus1)
    plus0 = add((late, 192), (low0, 0, 0, 24))
    minus0 = add((late, 240), (high0, 0, 24, 24))
    back, plus0, minus0 = together(back, plus0, minus0)
    from_left0, from_right0 = right(plus0), left(minus0)
    (last,) = call(
        last_kernel,
        [shape((128, 16, 128))],
        back,
        normal1,
        rstd1,
        message,
        mix_part,
        gain_part,
        scratch=[pltpu.VMEM((OWN, 16, 128), F32), pltpu.VMEM((16, 128), F32)],
    )
    from_left1, from_right1, last = together(from_left1, from_right1, last)
    over = add((late, 48), (from_left1, 0), (from_right1, 0))
    other = across(over)
    last = exchange(last, ALL)
    up_kept, down_kept, sent = call(
        split_kernel,
        [shape((128, 512)), shape((512, 256)), shape((384, 512))],
        place,
        add((late, 0), (from_left0, 0), (from_right0, 0)),
        other,
        scratch=add_scratch(2),
        scalars=1,
        remote_in=2,
        room=60,
    )
    up_grad, down_grad, gain_grad, mix_grad, proj_grad = call(
        finish_kernel,
        [
            shape((128, 1024)),
            shape((1024, 256)),
            shape((1, 128), F32),
            shape((12, 128), F32),
            shape((16, 16), F32),
        ],
        place,
        up_kept,
        down_kept,
        sibling(sent),
        last,
        scalars=1,
    )
    (layer_out,) = call(unfold_kernel, [shape((8, OWN, 16, 128))], back)
    gain_grad, mix_grad = gain_grad.reshape(128), mix_grad.T
    layer_out = layer_out.reshape(160, 16, 128)
    return (layer_out, gain_grad, mix_grad, up_grad, down_grad, proj_grad)


def solution(mesh):
    grid = Mesh(mesh.devices.reshape(2, 4, 2, 2, 4), ALL)
    placed = (
        P(DP, FEAT, None),
        P(FEAT, None),
        P(DP, FEAT),
        P(FEAT, DP),
        P(None, FEAT),
        P(),
        P(DP, FEAT, None),
    )
    return jax.shard_map(
        per_device,
        mesh=grid,
        in_specs=placed,
        out_specs=(
            P(DP, FEAT, None),
            P(),
            P(None, FEAT),
            P(DP, FEAT),
            P(FEAT, DP),
            P(FEAT, None),
        ),
        check_vma=False,
    )
```

```python
import functools

import jax
import jax.numpy as jnp
from jax import lax
from jax.experimental import pallas as pl
from jax.experimental.pallas import tpu as pltpu
from jax.sharding import Mesh, PartitionSpec as P

BF = jnp.bfloat16
F32 = jnp.float32
DP = ("zlo", "x", "core")
FEAT = ("zhi", "y")
ALL = DP + FEAT
EPS = 1e-05
FWD = [(i, (i + 1) % 4) for i in range(4)]
BWD = [(i, (i + 3) % 4) for i in range(4)]
SWAP = [(0, 1), (1, 0)]
OWN, CORE, CHIP = 20, 160, 320


def sibling(a):
    return lax.ppermute(a, "core", SWAP)


def across(a):
    return lax.ppermute(a, "zlo", SWAP)


def right(a):
    return lax.ppermute(a, "x", FWD)


def left(a):
    return lax.ppermute(a, "x", BWD)


def exchange(a, axes):
    return lax.all_to_all(a, axes, 0, 0, tiled=True)


def together(*arrays):
    return lax.optimization_barrier(arrays)


def dot(a, b, dims):
    return lax.dot_general(a, b, (dims, ((), ())), preferred_element_type=F32)


def shape(dims, dtype=BF):
    return jax.ShapeDtypeStruct(dims, dtype)


def call(body, outs, *args, scratch=(), scalars=0, remote_in=0, remote_out=0, room=16):
    whole = pl.BlockSpec(memory_space=pltpu.VMEM)
    small = pl.BlockSpec(memory_space=pltpu.SMEM)
    there = pl.BlockSpec(memory_space=pltpu.HBM)
    return pl.pallas_call(
        body,
        out_shape=outs,
        in_specs=[small] * scalars
        + [whole] * (len(args) - scalars - remote_in)
        + [there] * remote_in,
        out_specs=[there] * remote_out + [whole] * (len(outs) - remote_out),
        scratch_shapes=list(scratch),
        compiler_params=pltpu.CompilerParams(vmem_limit_bytes=room * 1024 * 1024),
    )(*args)


def one_where(dims, test):
    rows = lax.broadcasted_iota(jnp.int32, dims, 0)
    cols = lax.broadcasted_iota(jnp.int32, dims, 1)
    return test(rows, cols).astype(F32).astype(BF)


def many(start, size):
    return pl.ds(pl.multiple_of(start, size), size)


def halves(core, width):
    return many(core * width, width), many((1 - core) * width, width)


def chip_rows(core):
    return one_where((256, 128), lambda r, c: r == (c % 16) * 16 + core * 8 + c // 16)


def send_kernel(place, up, down, sent, sems):
    unused, other = halves(place[0], 512)
    low, high = many((1 - place[0]) * 512, 256), many((1 - place[0]) * 512 + 256, 256)
    copies = [
        pltpu.make_async_copy(up.at[:, other], sent.at[pl.ds(0, 128)], sems.at[0]),
        pltpu.make_async_copy(
            down.at[low], sent.at[pl.ds(128, 256), pl.ds(0, 256)], sems.at[1]
        ),
        pltpu.make_async_copy(
            down.at[high], sent.at[pl.ds(128, 256), pl.ds(256, 256)], sems.at[2]
        ),
    ]
    for copy in copies:
        copy.start()
    for copy in copies:
        copy.wait()


def message_kernel(place, proj, mix, emb, message, sems):
    copy = pltpu.make_async_copy(emb, message.at[:, pl.ds(0, 320)], sems.at[0])
    copy.start()
    here = one_where((16, 128), lambda n, lane: lane == place[3] * 16 + n)
    proj_rows = dot(proj[...], here, ((0,), (0,))).astype(BF)
    shift = one_where((16, 12), lambda u, c: u == c + 4)
    mix_rows = dot(shift, mix[...], ((1,), (0,))).astype(BF)
    for group in range(8):
        message[group, 320:336] = proj_rows
        message[group, 336:352] = mix_rows
    copy.wait()


def piece_kernel(place, got, up, down, out, token, piece, mine_up, mine_down, sems):
    core = place[0]
    token[...] = got[:16, :128]
    mine, unused = halves(core, 512)
    copies = [
        pltpu.make_async_copy(up.at[:, mine], mine_up, sems.at[0]),
        pltpu.make_async_copy(down.at[mine], mine_down, sems.at[1]),
    ]
    for copy in copies:
        copy.start()
    mine_at, other_at = halves(core, 256)
    piece[16:32, :, other_at] = got[128:, :256].reshape(16, 16, 256)
    piece[32:, :, other_at] = got[128:, 256:].reshape(16, 16, 256)
    rows = dot(chip_rows(1 - core), got[:128], ((1,), (0,)))
    copies[0].wait()
    rows += dot(chip_rows(core), mine_up[...], ((1,), (0,)))
    piece[:16] = rows.astype(BF).reshape(16, 16, 512)
    copies[1].wait()
    piece[16:, :, mine_at] = mine_down[...].reshape(32, 16, 256)
    copy = pltpu.make_async_copy(piece, out, sems.at[2])
    copy.start()
    copy.wait()


def total_of(refs):
    total = refs[0][...].astype(F32)
    for ref in refs[1:]:
        total += ref[...].astype(F32)
    return total.astype(BF)


def add_kernel(parts, *refs):
    *terms, out, held, total, sems, out_sems = refs
    sends, taken = [], {}
    for step in range(0, 48, 12):
        taken[step] = []
        for i, (start, first, count) in enumerate(parts):
            if first <= step < first + count:
                there = terms[i].at[pl.ds(start + step - first, 12)]
                sem = sems.at[step // 12 * len(parts) + i]
                copy = pltpu.make_async_copy(there, held.at[i, pl.ds(step, 12)], sem)
                copy.start()
                taken[step].append((i, copy))
    for step in range(0, 48, 12):
        at = slice(step, step + 12)
        part = jnp.zeros((12, 16, 512), F32)
        for i, copy in taken[step]:
            copy.wait()
            part += held[i, at].astype(F32)
        total[at] = part.astype(BF)
        if out is not None:
            at = pl.ds(step, 12)
            sem = out_sems.at[step // 12]
            sends.append(pltpu.make_async_copy(total.at[at], out.at[at], sem))
            sends[-1].start()
    for copy in sends:
        copy.wait()


def add_scratch(terms):
    return [
        pltpu.VMEM((terms, 48, 16, 512), BF),
        pltpu.VMEM((48, 16, 512), BF),
        pltpu.SemaphoreType.DMA((4 * terms,)),
        pltpu.SemaphoreType.DMA((4,)),
    ]


def add(*parts):
    parts = [(array, start, *(where or (0, 48))) for array, start, *where in parts]
    terms = [array for array, *unused in parts]
    return call(
        functools.partial(add_kernel, [where for unused, *where in parts]),
        [shape((48, 16, 512))],
        *terms,
        scratch=add_scratch(len(terms)),
        remote_in=len(terms),
        remote_out=1,
        room=60,
    )[0]


def sum_kernel(*refs):
    refs[-1][...] = total_of(refs[:-1])


def join_kernel(own, got, layer, out):
    out[:, :16] = total_of((own, got))
    out[:, 16:] = layer[...]


def split_kernel(place, one, two, up_kept, down_kept, sent, held, total, *sems):
    core = place[0]
    add_kernel([(0, 0, 48)] * 2, one, two, None, held, total, *sems)
    total = total[...]
    up, down = total[:16].reshape(256, 512), total[16:].reshape(512, 512)
    up_kept[...] = dot(chip_rows(core), up, ((0,), (0,))).astype(BF)
    sent[:128] = dot(chip_rows(1 - core), up, ((0,), (0,))).astype(BF)
    first, second = down[:, :256], down[:, 256:]
    down_kept[...] = jnp.where(core == 0, first, second)
    other = jnp.where(core == 0, second, first)
    sent[128:, :256] = other[:256]
    sent[128:, 256:] = other[256:]


def finish_kernel(place, up_kept, down_kept, got, last, up, down, gain, mix, proj):
    mine, other = halves(place[0], 512)
    up[:, mine] = up_kept[...]
    up[:, other] = got[:128]
    down[mine, :] = down_kept[...]
    down[other, :] = jnp.concatenate([got[128:, :256], got[128:, 256:]], 0)
    total = jnp.sum(last[...].astype(F32), axis=0)
    gain[...] = total[2:3]
    mix[...] = total[4:]
    token = lax.broadcasted_iota(jnp.int32, (16, 128), 0)
    lane = lax.broadcasted_iota(jnp.int32, (16, 128), 1)
    rows = jnp.where(token < 8, total[0:1], total[1:2])
    rows = jnp.where(token % 8 == lane // 16, rows, 0.0)
    pick = one_where((128, 16), lambda r, k: r % 16 == k).astype(F32)
    proj[...] = jnp.dot(
        rows, pick, precision=lax.Precision.HIGHEST, preferred_element_type=F32
    )


def unpack(ref, width, start, size):
    quarter = start // (width // 4)
    tail = width + start - quarter * (width // 4)
    rest = ref[:, :16, tail : tail + size].astype(F32)
    rest = [rest[f, 4 * quarter : 4 * quarter + 4] for f in range(8)]
    rest = jnp.concatenate(rest, 0).astype(BF)
    return [ref[:, :16, start : start + size].reshape(128, size), rest]


def pack(part, ref, tails, width, start, size):
    quarter = start // (width // 4)
    tail = start - quarter * (width // 4)
    ref[:, :, start : start + size] = part[:128].astype(BF).reshape(8, 16, size)
    for f in range(8):
        row = 16 * f + 4 * quarter
        tails[row : row + 4, tail : tail + size] = part[128 + 4 * f : 132 + 4 * f]
    if quarter == 3:
        rest = tails[:, tail : tail + size].astype(BF)
        ref[:, :, width + tail : width + tail + size] = rest.reshape(8, 16, size)


def chip_of(place, r):
    return jnp.bitwise_xor(place[1], r // 4) * 4 + lax.rem(place[2] + r % 4, 4)


def fetch(place, pieces, first_held, second_held, sems):
    first, second = [], []
    for r, piece in enumerate(pieces):
        at = first_held.at[:, many(chip_of(place, r) * 16, 16)]
        first.append(pltpu.make_async_copy(piece.at[pl.ds(0, 16)], at, sems.at[r]))
        copy = pltpu.make_async_copy(piece.at[pl.ds(16, 32)], second_held.at[r], sems.at[8 + r])
        second.append(copy)
    return first, second


def features_kernel(message, payload, normal, rstds, tails):
    proj_w = message[0, 320:336].astype(F32)
    for f in range(1, 8):
        proj_w += message[f, 320:336].astype(F32)
    proj_w = proj_w.astype(BF)

    def sample(b, carry):
        tokens = message[:, many(b * 16, 16)].reshape(128, 128)
        proj = dot(proj_w, tokens, ((1,), (0,))).astype(BF)
        inter = dot(proj, tokens, ((1,), (1,)))
        cent = inter - jnp.sum(inter, keepdims=True) * (1.0 / 2048)
        rstd = lax.rsqrt(jnp.sum(cent * cent, keepdims=True) * (1.0 / 2048) + EPS)
        normal[b] = cent * rstd
        rstds[b] = jnp.broadcast_to(rstd, (16, 128))
        return carry

    lax.fori_loop(0, OWN, sample, 0, unroll=20)
    for k in range(16):
        block = normal[:, k, :]
        quarter, tail = k // 4 * 4, k % 4 * 128
        tails[quarter : quarter + 4, tail : tail + 128] = block[16:]
        block = block[:16].astype(BF)
        for f in range(8):
            payload[f, :, 128 * k : 128 * k + 128] = block
    block = tails[...].astype(BF)
    for f in range(8):
        payload[f, :, 2048:] = block


def forward_kernel(place, own, sib, *refs):
    hidden, pre, rows, held, held_down, fmb_own, fmb_sib, tail_own, tail_sib, sems = refs[8:]
    first, second = fetch(place, refs[:8], held, held_down, sems)
    for copy in first + second:
        copy.start()
    for j in range(8):
        part = unpack(own, 2048, 256 * j, 256) + unpack(sib, 2048, 256 * j, 256)
        rows[:, 256 * j : 256 * j + 256] = jnp.concatenate(part, 0)
    for copy in first:
        copy.wait()
    total = dot(rows[...], held[...].reshape(2048, 512), ((1,), (0,)))
    pre[...] = total
    act = (total / (1.0 + jnp.exp(-total))).astype(BF)
    hidden[...] = act
    for copy in second:
        copy.wait()
    for r in range(8):
        part = dot(act, held_down[r].reshape(512, 512), ((1,), (0,)))
        pack(part[:CORE], fmb_own, tail_own, 4096, 512 * r, 512)
        pack(part[CORE:], fmb_sib, tail_sib, 4096, 512 * r, 512)


def backward_kernel(place, d_own, d_sib, rows, hidden, pre, held, held_down, *refs):
    far1_low, far1_high, far0_low, far0_high, late, dn_own, dn_sib = refs[:7]
    d_rows, made, made_down, tail_own, tail_sib, out_sems = refs[7:]
    halves_of = {2: (far0_low, far0_high), 6: (far1_low, far1_high)}
    starts = {0: 0, 4: 48, 5: 96, 7: 144, 1: 192, 3: 240}
    total = jnp.zeros((CHIP, 512), F32)
    for r in range(8):
        part = unpack(d_own, 4096, 512 * r, 512) + unpack(d_sib, 4096, 512 * r, 512)
        part = jnp.concatenate(part, 0)
        d_rows[:, 512 * r : 512 * r + 512] = part
        total += dot(part, held_down[r].reshape(512, 512), ((1,), (1,)))
    sends = []

    def send(source, there, sem):
        sends.append(pltpu.make_async_copy(source, there, out_sems.at[sem]))
        sends[-1].start()

    act = hidden[...].T
    for r in (6, 7, 2, 5, 4, 1, 3, 0):
        part = dot(act, d_rows[:, 512 * r : 512 * r + 512], ((1,), (0,)))
        made_down[r] = part.astype(BF).reshape(32, 16, 512)
        if r in halves_of:
            low, high = halves_of[r]
            send(made_down.at[r, pl.ds(0, 8)], low.at[pl.ds(16, 8)], 8 + r)
            send(made_down.at[r, pl.ds(8, 24)], high, 16 + r // 4)
        else:
            send(made_down.at[r], late.at[pl.ds(starts[r] + 16, 32)], 8 + r)
    sig = 1.0 / (1.0 + jnp.exp(-pre[...]))
    d_pre = (total * (sig * (1.0 + pre[...] * (1.0 - sig)))).astype(BF)
    for j in range(8):
        part = dot(rows[:, 256 * j : 256 * j + 256], d_pre, ((0,), (0,)))
        made[2 * j : 2 * j + 2] = part.astype(BF).reshape(2, 128, 512)
    for r in range(8):
        there = halves_of[r][0] if r in halves_of else late.at[pl.ds(starts[r], 48)]
        here = made.at[:, many(chip_of(place, r) * 16, 16)]
        send(here, there.at[pl.ds(0, 16)], r)
    for j in range(8):
        part = dot(d_pre, held[2 * j : 2 * j + 2].reshape(256, 512), ((1,), (1,)))
        pack(part[:CORE], dn_own, tail_own, 2048, 256 * j, 256)
        pack(part[CORE:], dn_sib, tail_sib, 2048, 256 * j, 256)
    for copy in sends:
        copy.wait()


def norm_kernel(
    place, parts, message, cot, gain, layer, d_fmb, mix_part, gain_part, fm, grad, tails
):
    def added(cols):
        total = parts[0, :, cols].astype(F32)
        for f in range(1, 8):
            total += parts[f, :, cols].astype(F32)
        return total

    fm[...] = jnp.zeros_like(fm)
    tails[...] = added(slice(4096, 5120))
    for r in range(8):
        main = added(slice(512 * r, 512 * r + 512))
        quarter, tail = r // 2 * 4, r % 2 * 512
        for u in range(4):
            at = slice(128 * u, 128 * u + 128)
            fm[:16, chip_of(place, r), u, :] = main[:, at]
            at = slice(tail + 128 * u, tail + 128 * u + 128)
            fm[16:, chip_of(place, r), u, :] = tails[quarter : quarter + 4, at]
    mix_part[...] = jnp.zeros_like(mix_part)
    gain_part[...] = jnp.zeros_like(gain_part)
    scale = gain[...]
    mixing = message[:, 336:352].reshape(128, 128)

    def mean(a):
        return jnp.sum(a, axis=1, keepdims=True) * (1.0 / 128)

    def sample(b, carry):
        at = many(b * 16, 16)
        tokens = message[:, at].reshape(128, 128)
        cotan = cot[:, at].reshape(128, 128).astype(F32)
        lcb = dot(mixing, tokens, ((1,), (0,)))
        summed = lcb + fm[b].reshape(128, 128) + tokens.astype(F32)
        cent = summed - mean(summed)
        rstd = lax.rsqrt(mean(cent * cent) + EPS)
        normal = cent * rstd
        layer[:, :, many(b * 128, 128)] = (normal * scale).astype(BF).reshape(8, 16, 128)
        gain_part[...] += jnp.sum((cotan * normal).reshape(16, 8, 128), axis=0)
        dnorm = cotan * scale
        dsum = rstd * (dnorm - mean(dnorm) - normal * mean(dnorm * normal))
        grad[b] = dsum.reshape(8, 16, 128)
        mix_part[...] += dot(dsum.astype(BF), tokens, ((1,), (1,)))
        return carry

    lax.fori_loop(0, OWN, sample, 0, unroll=20)
    for r in range(8):
        quarter, tail = r // 2 * 4, r % 2 * 512
        for u in range(4):
            block = grad[:, chip_of(place, r), u, :]
            at = slice(tail + 128 * u, tail + 128 * u + 128)
            tails[quarter : quarter + 4, at] = block[16:]
            block = block[:16].astype(BF)
            for f in range(8):
                d_fmb[f, :, 512 * r + 128 * u : 512 * r + 128 * u + 128] = block
    block = tails[...].astype(BF)
    for f in range(8):
        d_fmb[f, :, 4096:] = block


def last_kernel(back, normal, rstds, message, mix_part, gain_part, last, grad, proj_part):
    total = back[0, :16].astype(F32)
    for f in range(1, 8):
        total += back[f, :16].astype(F32)
    for k in range(16):
        quarter, tail = k // 4 * 4, 2048 + k % 4 * 128
        grad[:16, k, :] = total[:, 128 * k : 128 * k + 128]
        grad[16:, k, :] = total[quarter : quarter + 4, tail : tail + 128]
    proj_part[...] = jnp.zeros_like(proj_part)

    def sample(b, carry):
        tokens = message[:, many(b * 16, 16)].reshape(128, 128)
        d_normed, norm = grad[b], normal[b]
        first = jnp.sum(d_normed, keepdims=True) * (1.0 / 2048)
        second = jnp.sum(d_normed * norm, keepdims=True) * (1.0 / 2048)
        d_inter = rstds[b] * (d_normed - first - norm * second)
        d_proj = dot(d_inter.astype(BF), tokens, ((1,), (0,)))
        proj_part[...] += dot(d_proj.astype(BF), tokens, ((1,), (1,)))
        return carry

    lax.fori_loop(0, OWN, sample, 0, unroll=20)
    repeat = one_where((16, 128), lambda k, lane: lane % 16 == k)
    spread = dot(proj_part[...].astype(BF), repeat, ((0,), (0,)))
    token = lax.broadcasted_iota(jnp.int32, (128, 128), 0)
    lane = lax.broadcasted_iota(jnp.int32, (128, 128), 1)
    spread = jnp.where(token % 8 == lane // 16, spread, 0.0).astype(BF)
    collect = one_where(
        (128, 128), lambda r, n: (r % 16 < 2) & (n // 8 == (r // 16) * 2 + r % 16)
    )
    rows = dot(collect, spread, ((1,), (0,)))
    gain = jnp.sum(gain_part[...], axis=0, keepdims=True)
    rows += jnp.where(token % 16 == 2, jnp.broadcast_to(gain, (128, 128)), 0.0)
    rows += jnp.where(token % 16 >= 4, mix_part[...], 0.0)
    rows = rows.astype(BF).reshape(8, 16, 128)
    for d in range(16):
        last[8 * d : 8 * d + 8] = rows


def unfold_kernel(back, layer):
    for b in range(OWN):
        layer[:, b] = back[:, 16:, 128 * b : 128 * b + 128]


def per_device(embeddings, proj_weight, up_weight, down_weight, mix_weight, out_gain, cotangent):
    place = jnp.stack(
        [lax.axis_index(axis) for axis in ("core", "zlo", "x")]
        + [lax.axis_index("zhi") * 4 + lax.axis_index("y")]
    ).astype(jnp.int32)
    (sent,) = call(
        send_kernel,
        [shape((384, 512))],
        place,
        up_weight,
        down_weight,
        scratch=[pltpu.SemaphoreType.DMA((3,))],
        scalars=1,
        remote_in=2,
    )
    mine, token = call(
        piece_kernel,
        [shape((48, 16, 512)), shape((16, 128))],
        place,
        sibling(sent),
        up_weight,
        down_weight,
        scratch=[
            pltpu.VMEM((48, 16, 512), BF),
            pltpu.VMEM((128, 512), BF),
            pltpu.VMEM((512, 256), BF),
            pltpu.SemaphoreType.DMA((3,)),
        ],
        scalars=1,
        remote_in=2,
        remote_out=1,
    )
    other = across(mine)
    near_left, near_right = right(mine), left(mine)
    (message,) = call(
        message_kernel,
        [shape((8, 352, 128))],
        place,
        proj_weight,
        mix_weight.T,
        embeddings.reshape(8, 320, 128),
        scratch=[pltpu.SemaphoreType.DMA((1,))],
        scalars=1,
        remote_in=1,
    )
    message, token = together(message, sibling(token))
    message = exchange(message, FEAT)
    message, near_left, near_right, other = together(message, near_left, near_right, other)
    other_left, other_right = right(other), left(other)

    payload, normal1, rstd1 = call(
        features_kernel,
        [shape((8, 16, 2560)), shape((OWN, 16, 128), F32), shape((OWN, 16, 128), F32)],
        message,
        scratch=[pltpu.VMEM((16, 512), F32)],
    )
    payload, cotangent = together(payload, cotangent)
    cotan = exchange(cotangent.reshape(8, 320, 128), FEAT)
    payload, cotan, token, near_left, other_left, other_right = together(
        payload, cotan, token, near_left, other_left, other_right
    )
    far, other_far = right(near_left), left(other_right)
    payload, token = together(payload, sibling(token))
    normed = exchange(payload, FEAT)
    normed, far, other_far = together(normed, far, other_far)
    weights = [mine, near_right, far, near_left, other, other_right, other_far, other_left]
    hidden, pre, rows, first, second, fmb_own, fmb_sib = call(
        forward_kernel,
        [
            shape((CHIP, 512)),
            shape((CHIP, 512), F32),
            shape((CHIP, 2048)),
            shape((16, 128, 512)),
            shape((8, 32, 16, 512)),
            shape((8, 16, 5120)),
            shape((8, 16, 5120)),
        ],
        place,
        normed,
        sibling(normed),
        *weights,
        scratch=[
            pltpu.VMEM((128, 1024), F32),
            pltpu.VMEM((128, 1024), F32),
            pltpu.SemaphoreType.DMA((16,)),
        ],
        scalars=1,
        remote_in=8,
    )
    (fmb,) = call(sum_kernel, [shape((8, 16, 5120))], fmb_own, sibling(fmb_sib))
    fmb = exchange(fmb, FEAT)

    layer_out, d_fmb, mix_part, gain_part = call(
        norm_kernel,
        [
            shape((8, 16, 2560)),
            shape((8, 16, 5120)),
            shape((128, 128), F32),
            shape((8, 128), F32),
        ],
        place,
        fmb,
        message,
        cotan,
        out_gain.reshape(1, 128),
        scratch=[
            pltpu.VMEM((OWN, 8, 16, 128), F32),
            pltpu.VMEM((OWN, 8, 16, 128), F32),
            pltpu.VMEM((16, 1024), F32),
        ],
        scalars=1,
    )

    d_fmb = exchange(d_fmb, FEAT)
    far1_low, far1_high, far0_low, far0_high, late, dn_own, dn_sib = call(
        backward_kernel,
        [shape((24, 16, 512))] * 4 + [shape((288, 16, 512))] + [shape((8, 16, 2560))] * 2,
        place,
        d_fmb,
        sibling(d_fmb),
        rows,
        hidden,
        pre,
        first,
        second,
        scratch=[
            pltpu.VMEM((CHIP, 4096), BF),
            pltpu.VMEM((16, 128, 512), BF),
            pltpu.VMEM((8, 32, 16, 512), BF),
            pltpu.VMEM((128, 512), F32),
            pltpu.VMEM((128, 512), F32),
            pltpu.SemaphoreType.DMA((18,)),
        ],
        scalars=1,
        remote_out=5,
        room=36,
    )

    low1, high1 = right(far1_low), left(far1_high)
    low0, high0 = right(far0_low), left(far0_high)
    (back,) = call(join_kernel, [shape((8, 32, 2560))], dn_own, sibling(dn_sib), layer_out)
    back = exchange(back, FEAT)
    plus1 = add((late, 96), (low1, 0, 0, 24))
    minus1 = add((late, 144), (high1, 0, 24, 24))
    plus1, minus1, low0, high0 = together(plus1, minus1, low0, high0)
    from_left1, from_right1 = right(plus1), left(minus1)
    plus0 = add((late, 192), (low0, 0, 0, 24))
    minus0 = add((late, 240), (high0, 0, 24, 24))
    back, plus0, minus0 = together(back, plus0, minus0)
    from_left0, from_right0 = right(plus0), left(minus0)
    (last,) = call(
        last_kernel,
        [shape((128, 16, 128))],
        back,
        normal1,
        rstd1,
        message,
        mix_part,
        gain_part,
        scratch=[pltpu.VMEM((OWN, 16, 128), F32), pltpu.VMEM((16, 128), F32)],
    )
    from_left1, from_right1, last = together(from_left1, from_right1, last)
    over = add((late, 48), (from_left1, 0), (from_right1, 0))
    other = across(over)
    last = exchange(last, ALL)
    up_kept, down_kept, sent = call(
        split_kernel,
        [shape((128, 512)), shape((512, 256)), shape((384, 512))],
        place,
        add((late, 0), (from_left0, 0), (from_right0, 0)),
        other,
        scratch=add_scratch(2),
        scalars=1,
        remote_in=2,
        room=60,
    )
    up_grad, down_grad, gain_grad, mix_grad, proj_grad = call(
        finish_kernel,
        [
            shape((128, 1024)),
            shape((1024, 256)),
            shape((1, 128), F32),
            shape((12, 128), F32),
            shape((16, 16), F32),
        ],
        place,
        up_kept,
        down_kept,
        sibling(sent),
        last,
        scalars=1,
    )
    (layer_out,) = call(unfold_kernel, [shape((8, OWN, 16, 128))], back)
    gain_grad, mix_grad = gain_grad.reshape(128), mix_grad.T
    layer_out = layer_out.reshape(160, 16, 128)
    return (layer_out, gain_grad, mix_grad, up_grad, down_grad, proj_grad)


def solution(mesh):
    grid = Mesh(mesh.devices.reshape(2, 4, 2, 2, 4), ALL)
    placed = (
        P(DP, FEAT, None),
        P(FEAT, None),
        P(DP, FEAT),
        P(FEAT, DP),
        P(None, FEAT),
        P(),
        P(DP, FEAT, None),
    )
    return jax.shard_map(
        per_device,
        mesh=grid,
        in_specs=placed,
        out_specs=(
            P(DP, FEAT, None),
            P(),
            P(None, FEAT),
            P(DP, FEAT),
            P(FEAT, DP),
            P(FEAT, None),
        ),
        check_vma=False,
    )
```
